768 devices in a mesh: dp: 48 (over x, z_lo, core), expert: 2 (over z_hi), tensor: 8 (over y).
Axes of the slice: x: 4, y: 8, z: 12 (z_hi: 2, z_lo: 6; z = z_hi * 6 + z_lo), core: 2. Of those that a mesh axis runs over, the one named last changes fastest.
Arguments:
- routes: int32 [98304, 2], P(('dp', 'expert', 'tensor')), may hold values from 0 to 7, as said below
- upgrad: bfloat16 [48, 2, 8, 2, 40, 8192], P('dp', 'expert', None, None, None, 'tensor'), may hold values from -6 to 6
- weight: bfloat16 [2, 3072, 8192], P('expert', 'dp', 'tensor'), may hold values from -0.0625 to 0.0625
Outputs:
- input_grad: bfloat16 [98304, 3072], P(('dp', 'expert', 'tensor'))
The draws below stay inside these ranges and needn't reach their ends.
Inputs may be any that keep to these rules, and one draw needn't show every extreme that they name: `routes`: each row names two different experts. In the rows of one device, each expert whose number is below the size of the expert axis is named by at most 40 rows, and in every group of devices with one dp index one such expert is named by exactly 40 rows on each of its devices.
All inputs are finite; a program needn't handle non-finite values.
Results may differ from the reference program's by a relative error of at most 0.018.
Values may be sent and summed in bfloat16 or wider, within the bound.
No kernel may reach another device: no remote copies, remote signals or barrier semaphores. Data moves between devices by JAX's collectives and lax.ppermute only.
A program may use at most 32 MiB of HBM per device.

```python
import jax
import jax.numpy as jnp
from jax import lax

DW = 3072
FF_DEV = 1024
EXPERTS = 8
TOK_DEV = 128
CAP = 40
FF = 8192
TOKENS = 98304
N_DP = 48
N_EXPERT = 2
N_TENSOR = 8


def draw_routes(key, part):
    key = jax.random.fold_in(key, 11)
    block_count = TOKENS // TOK_DEV
    group_size = N_EXPERT * N_TENSOR
    key_full, key_count, key_order, key_other, key_step, key_swap = jax.random.split(key, 6)
    full_group = jax.random.randint(key_full, (block_count // group_size,), 0, N_EXPERT)
    full_block = jnp.repeat(full_group, group_size)
    row_counts = jax.random.randint(key_count, (block_count, N_EXPERT), 1, CAP + 1)
    expert_ids = jnp.arange(N_EXPERT)
    row_counts = jnp.where(full_block[:, None] == expert_ids[None, :], CAP, row_counts)
    order_keys = jax.random.split(key_order, block_count * N_EXPERT)
    orderings = jax.vmap(lambda single: jax.random.permutation(single, TOK_DEV))(order_keys)
    orderings = orderings.reshape(block_count, N_EXPERT, TOK_DEV)
    rank_of = jnp.argsort(orderings, axis=-1)
    members = rank_of < row_counts[:, :, None]
    in_first = members[:, 0, :]
    in_second = members[:, 1, :]
    other_one = jax.random.randint(key_other, (block_count, TOK_DEV), N_EXPERT, EXPERTS)
    offset_step = jax.random.randint(key_step, (block_count, TOK_DEV), 1, EXPERTS - N_EXPERT)
    other_two = N_EXPERT + (other_one - N_EXPERT + offset_step) % (EXPERTS - N_EXPERT)
    first_pick = jnp.where(in_first, 0, jnp.where(in_second, 1, other_one))
    second_pick = jnp.where(in_first & in_second, 1, jnp.where(in_first | in_second, other_one, other_two))
    swapped = jax.random.randint(key_swap, (block_count, TOK_DEV), 0, 2) == 1
    column_one = jnp.where(swapped, second_pick, first_pick)
    column_two = jnp.where(swapped, first_pick, second_pick)
    return jnp.stack([column_one, column_two], axis=-1).reshape(TOKENS, 2).astype(jnp.int32)


def shard_levels(rng, extent, shards, low, top_value):
    def one(position, blocks):
        heights = jax.random.uniform(jax.random.fold_in(jax.random.fold_in(rng, 6), position), (blocks,), jnp.float32, low / len(shards), top_value / len(shards))
        return jnp.repeat(jnp.exp(heights), extent[position] // blocks).reshape((-1,) + (1,) * (len(extent) - position - 1))

    loudness = one(*shards[0])
    for cut in shards[1:]:
        loudness = loudness * one(*cut)
    return loudness


def gaussian(own_key, shape, spread, bound, pieces=(), kind=jnp.bfloat16):
    values = jax.random.normal(own_key, shape, jnp.float32) * spread
    if len(pieces) > 0:
        values = shard_levels(own_key, shape, pieces, -0.22, 0.18) * values
    return jnp.clip(values, min=-bound, max=bound).astype(kind)


def setup_inputs(seed: int = 0) -> dict:
    seeds = jax.random.split(jax.random.key(seed), 4)
    routes = draw_routes(jax.random.fold_in(seeds[3], 71), 0)
    upgrad = gaussian(seeds[1], (N_DP, N_EXPERT, N_TENSOR, N_EXPERT, CAP, FF), 1.0, 6.0, ((0, 48), (1, 2), (5, 8)))
    weight = gaussian(seeds[2], (N_EXPERT, DW, FF), FF ** -0.5, 0.0625, ((0, 2), (1, 48), (2, 8)))
    return {"routes": routes, "upgrad": upgrad, "weight": weight}


def reference(routes, upgrad, weight):
    row_total = N_TENSOR * N_EXPERT * CAP
    experts_here = jnp.arange(N_EXPERT, dtype=jnp.int32)
    positions = jnp.arange(CAP, dtype=jnp.int32)

    def per_group(inputs):
        grad_block, choices = inputs
        returned_rows = []
        for expert_id in range(N_EXPERT):
            row_block = grad_block[expert_id].reshape(row_total, N_TENSOR, FF_DEV).astype(jnp.float32)
            weight_slab = weight[expert_id].reshape(DW, N_TENSOR, FF_DEV).astype(jnp.float32)
            partials = jnp.einsum('rjf,djf->jrd', row_block, weight_slab)
            rounded = lax.optimization_barrier(partials.astype(jnp.bfloat16))
            summed = jnp.sum(rounded.astype(jnp.float32), axis=0)
            returned_rows.append(summed.astype(jnp.bfloat16).reshape(N_TENSOR, N_EXPERT, CAP, DW))
        returned_all = jnp.stack(returned_rows)
        choices = choices.reshape(N_EXPERT, N_TENSOR, TOK_DEV, 2)
        is_routed = jnp.any(choices[..., None] == experts_here, axis=3)
        slot_index = jnp.cumsum(is_routed.astype(jnp.int32), axis=2) - 1
        onehot = is_routed[..., None] & (slot_index[..., None] == positions)
        combined = jnp.einsum('etias,atesd->etid', onehot.astype(jnp.float32), returned_all.astype(jnp.float32))
        return combined.astype(jnp.bfloat16)

    choices_all = routes.reshape(N_DP, N_EXPERT * N_TENSOR, TOK_DEV, 2)
    result = lax.map(per_group, (upgrad, choices_all))
    return result.reshape(TOKENS, DW)
```

```python
import jax
import jax.numpy as jnp
from jax import lax
from jax.experimental import pallas as pl
from jax.experimental.pallas import tpu as pltpu
from jax.sharding import PartitionSpec as P

NX, NZ, NC = 4, 6, 2
HALF = NZ // 2


def dp_index(x, z, c):
    return (x * NZ + z) * NC + c


def dp_perm(move):
    return [
        (dp_index(x, z, c), dp_index(*move(x, z, c)))
        for x in range(NX)
        for z in range(NZ)
        for c in range(NC)
    ]


SWAP_CORE = dp_perm(lambda x, z, c: (x, z, 1 - c))
SWAP_HALF = dp_perm(lambda x, z, c: (x, (z + HALF) % NZ, c))
TURN_UP = dp_perm(lambda x, z, c: (x, HALF * (z // HALF) + (z % HALF + 1) % HALF, c))
TURN_DOWN = dp_perm(lambda x, z, c: (x, HALF * (z // HALF) + (z % HALF - 1) % HALF, c))
X_UP = dp_perm(lambda x, z, c: ((x + 1) % NX, z, c))
X_DOWN = dp_perm(lambda x, z, c: ((x - 1) % NX, z, c))


def gather_weight(slab):
    move = lambda value, perm: lax.ppermute(value, "dp", perm)
    pair = jnp.stack([slab, move(slab, SWAP_HALF)])
    own = jnp.concatenate([pair, move(pair, TURN_UP), move(pair, TURN_DOWN)])
    below = move(own, X_UP)
    above = move(own, X_DOWN)
    far_first = move(below[:HALF], X_UP)
    far_last = move(above[HALF:], X_DOWN)
    return own, jnp.concatenate([below, above]), jnp.concatenate([far_first, far_last])


def block_places():
    dp = lax.axis_index("dp")
    z = (dp // NC) % NZ
    x = dp // (NC * NZ)
    half, m = z // HALF, z % HALF
    zs = []
    for turn in (0, -1, 1):
        at = (m + turn + HALF) % HALF
        zs += [half * HALF + at, (1 - half) * HALF + at]
    xs = [x, (x - 1 + NX) % NX, (x + 1) % NX, (x + 2) % NX]
    return jnp.stack([xi * NZ + zi for xi in xs for zi in zs]).astype(jnp.int32)


def sum_over_tensor(partial):
    n = partial.shape[0]
    mid = n // 2
    half_rows = partial.shape[1] // 2
    up = [(i, (i + 1) % n) for i in range(n)]
    down = [(i, (i - 1) % n) for i in range(n)]
    first = lax.ppermute(partial[mid, :half_rows], "tensor", up)
    last = lax.ppermute(partial[mid, half_rows:], "tensor", down)
    add = lambda a, b: (a.astype(jnp.float32) + b.astype(jnp.float32)).astype(jnp.bfloat16)
    going_up = jnp.concatenate([add(partial[mid - 1, :half_rows], first), partial[mid - 1, half_rows:]])
    going_down = jnp.concatenate([partial[mid + 1, :half_rows], add(partial[mid + 1, half_rows:], last)])
    for step in range(1, mid):
        from_below = lax.ppermute(going_up, "tensor", up)
        from_above = lax.ppermute(going_down, "tensor", down)
        if step < mid - 1:
            going_up = add(partial[mid - 1 - step], from_below)
            going_down = add(partial[mid + 1 + step], from_above)
    total = partial[0].astype(jnp.float32) + from_below.astype(jnp.float32) + from_above.astype(jnp.float32)
    return total.astype(jnp.bfloat16)


def exchange(summed, owners, capacity):
    features = summed.shape[-1]
    me = lax.axis_index("expert")
    rows = summed.reshape(NC, owners, capacity, features)
    keep = lax.dynamic_index_in_dim(rows, me, 1, keepdims=False)
    give = lax.dynamic_index_in_dim(rows, 1 - me, 1, keepdims=False)
    got = lax.ppermute(give, "expert", [(0, 1), (1, 0)])
    first = jnp.where(me == 0, keep, got)
    second = jnp.where(me == 0, got, keep)
    both = jnp.stack([first, second], axis=1).reshape(NC, owners * capacity, features)
    return both[0], lax.ppermute(both[1], "dp", SWAP_CORE)


def place_kernel(groups, width, places, core, onehot, *refs):
    out = refs[-1]
    first_core = core[0] == 0
    at = 0
    for g in range(groups):
        mine = jnp.dot(onehot[...], refs[2 * g][...], preferred_element_type=jnp.float32).astype(jnp.bfloat16)
        theirs = jnp.dot(onehot[...], refs[2 * g + 1][...], preferred_element_type=jnp.float32).astype(jnp.bfloat16)
        low = jnp.where(first_core, mine, theirs)
        high = jnp.where(first_core, theirs, mine)
        for b in range(mine.shape[1] // width):
            block = jnp.concatenate([low[:, b * width:(b + 1) * width], high[:, b * width:(b + 1) * width]], axis=1)
            start = pl.multiple_of(places[at] * (NC * width), NC * width)
            out[:, pl.ds(start, NC * width)] = block
            at += 1


def shards(routes, upgrad, weight):
    _, _, tensor_count, owners, capacity, hidden = upgrad.shape
    slab = weight[0]
    width = slab.shape[0]
    rows = owners * capacity
    me = lax.axis_index("tensor")
    dp = lax.axis_index("dp")

    own_rows = upgrad.reshape(tensor_count, rows, hidden)
    other_rows = lax.ppermute(own_rows, "dp", SWAP_CORE)
    turned = jnp.concatenate([own_rows, other_rows], axis=1)
    turned = jnp.concatenate([turned, turned], axis=0)
    turned = lax.dynamic_slice_in_dim(turned, me, tensor_count, 0)
    flat = turned.reshape(tensor_count * NC * rows, hidden)

    parts = []
    for blocks in gather_weight(slab):
        features = blocks.shape[0] * width
        partial = lax.dot_general(
            flat,
            blocks.reshape(features, hidden),
            (((1,), (1,)), ((), ())),
            preferred_element_type=jnp.float32,
        ).astype(jnp.bfloat16)
        summed = sum_over_tensor(partial.reshape(tensor_count, NC * rows, features))
        parts += exchange(summed, owners, capacity)

    owner_ids = lax.iota(jnp.int32, owners)
    is_routed = jnp.any(routes[:, :, None] == owner_ids[None, None, :], axis=1)
    slot_index = jnp.cumsum(is_routed.astype(jnp.int32), axis=0) - 1
    onehot = is_routed[:, :, None] & (slot_index[:, :, None] == lax.iota(jnp.int32, capacity)[None, None, :])
    onehot = onehot.reshape(routes.shape[0], rows).astype(jnp.bfloat16)

    smem = pl.BlockSpec(memory_space=pltpu.SMEM)
    vmem = pl.BlockSpec(memory_space=pltpu.VMEM)
    groups = len(parts) // 2

    def body(*refs):
        place_kernel(groups, width, *refs)

    return pl.pallas_call(
        body,
        out_shape=jax.ShapeDtypeStruct((routes.shape[0], NX * NZ * NC * width), jnp.bfloat16),
        in_specs=[smem, smem] + [vmem] * (1 + len(parts)),
        out_specs=vmem,
        compiler_params=pltpu.CompilerParams(vmem_limit_bytes=32 * 1024 * 1024),
    )(block_places(), (dp % NC).astype(jnp.int32).reshape(1), onehot, *parts)


def solution(mesh):
    return jax.shard_map(
        shards,
        mesh=mesh,
        in_specs=(
            P(("dp", "expert", "tensor"), None),
            P("dp", "expert", None, None, None, "tensor"),
            P("expert", "dp", "tensor"),
        ),
        out_specs=P(("dp", "expert", "tensor"), None),
        check_vma=False,
    )
```

```python
import jax
import jax.numpy as jnp
from jax import lax
from jax.experimental import pallas as pl
from jax.experimental.pallas import tpu as pltpu
from jax.sharding import Mesh, PartitionSpec as P

SIZES = {"x": 4, "h": 2, "m": 3, "c": 2, "e": 2, "q": 4, "p": 2}
GROUPS = ((0, 2), (2, 3))


def spread(value, axis):
    count = SIZES[axis]
    return lax.all_to_all(jnp.broadcast_to(value[None], (count,) + value.shape), axis, 0, 0)


def gather_weight(slab):
    width, hidden = slab.shape
    halves = slab.reshape(SIZES["p"], width // SIZES["p"], hidden)
    sent = jnp.broadcast_to(halves[None], (SIZES["h"],) + halves.shape)
    got = lax.all_to_all(sent.reshape((-1,) + halves.shape[1:]), ("h", "p"), 0, 0)
    got = got.reshape((SIZES["h"],) + halves.shape).transpose(0, 2, 1, 3)
    column = spread(got, "m")
    return [spread(column[low:high], "x") for low, high in GROUPS]


def gather_rows(own):
    def both(value, axis, at):
        other = lax.ppermute(value, axis, [(0, 1), (1, 0)])
        first = lax.axis_index(axis) == 0
        return jnp.stack([jnp.where(first, value, other), jnp.where(first, other, value)], axis=at)

    return both(both(own, "p", 2), "c", 1)


def place_kernel(out, onehot, pieces, width):
    columns = []
    count = SIZES["m"] * SIZES["h"]
    for x in range(SIZES["x"]):
        for z in range(count):
            h, m = z // SIZES["m"], z % SIZES["m"]
            for group, (low, high) in enumerate(GROUPS):
                if low <= m < high:
                    at = ((x * (high - low) + m - low) * SIZES["h"] + h) * width
                    for c in range(SIZES["c"]):
                        for p in range(SIZES["p"]):
                            columns.append(pieces[group][p * SIZES["c"] + c, :, at:at + width])
    tile = SIZES["c"] * SIZES["p"]
    for start in range(0, len(columns), tile):
        block = jnp.concatenate(columns[start:start + tile], axis=1)
        result = jnp.dot(onehot[...], block, preferred_element_type=jnp.float32)
        out[:, start * width:(start + tile) * width] = result.astype(out.dtype)


def shards(routes, upgrad, weight):
    _, _, tensor_count, owners, capacity, hidden = upgrad.shape
    slab = weight[0]
    width = slab.shape[0] // SIZES["p"]
    rows = owners * capacity

    weights = gather_weight(slab)
    grads = gather_rows(upgrad.reshape(tensor_count, rows, hidden))
    flat = grads.reshape(-1, SIZES["p"] * hidden)

    pieces = []
    for blocks in weights:
        blocks = blocks.reshape(-1, SIZES["p"] * hidden)
        features = blocks.shape[0]
        partial = lax.dot_general(
            flat, blocks, (((1,), (1,)), ((), ())), preferred_element_type=jnp.float32
        ).astype(jnp.bfloat16)
        parts = lax.all_to_all(partial.reshape(SIZES["q"], -1, features), "q", 0, 0)
        summed = jnp.sum(parts.astype(jnp.float32), axis=0).astype(jnp.bfloat16)
        returned = lax.all_to_all(summed.reshape(-1, capacity, features), ("p", "c", "e"), 0, 0)
        pieces.append(returned.reshape(-1, rows, features))

    owner_ids = lax.iota(jnp.int32, owners)
    is_routed = jnp.any(routes[:, :, None] == owner_ids[None, None, :], axis=1)
    slot_index = jnp.cumsum(is_routed.astype(jnp.int32), axis=0) - 1
    onehot = is_routed[:, :, None] & (slot_index[:, :, None] == lax.iota(jnp.int32, capacity)[None, None, :])
    onehot = onehot.reshape(routes.shape[0], rows).astype(jnp.bfloat16)

    def body(onehot_ref, *refs):
        place_kernel(refs[-1], onehot_ref, refs[:-1], width)

    vmem = pl.BlockSpec(memory_space=pltpu.VMEM)
    total = sum(piece.shape[0] * piece.shape[2] for piece in pieces)
    return pl.pallas_call(
        body,
        out_shape=jax.ShapeDtypeStruct((routes.shape[0], total), jnp.bfloat16),
        in_specs=[vmem] * (1 + len(pieces)),
        out_specs=vmem,
        compiler_params=pltpu.CompilerParams(vmem_limit_bytes=32 * 1024 * 1024),
    )(onehot, *pieces)


def solution(mesh):
    fine = Mesh(mesh.devices.reshape(tuple(SIZES.values())), tuple(SIZES))
    dp, tensor = ("x", "h", "m", "c"), ("q", "p")
    return jax.shard_map(
        shards,
        mesh=fine,
        in_specs=(
            P(dp + ("e",) + tensor, None),
            P(dp, "e", None, None, None, tensor),
            P("e", dp, tensor),
        ),
        out_specs=P(dp + ("e",) + tensor, None),
        check_vma=False,
    )
```

```python
import jax
import jax.numpy as jnp
from jax import lax
from jax.experimental import pallas as pl
from jax.experimental.pallas import tpu as pltpu
from jax.sharding import Mesh, PartitionSpec as P

SIZES = {"xh": 2, "xp": 2, "h": 2, "m": 3, "c": 2, "e": 2, "t": 8}
DP = ("xh", "xp", "h", "m", "c")
SWAP = [(0, 1), (1, 0)]
WEIGHT_SWAP = [(i, 3 - i) for i in range(4)]


def turn(shift):
    return [(i, (i + shift) % SIZES["m"]) for i in range(SIZES["m"])]


def gather_column(slab):
    pair = jnp.stack([slab, lax.ppermute(slab, "h", SWAP)])
    return jnp.concatenate([pair, lax.ppermute(pair, "m", turn(1)), lax.ppermute(pair, "m", turn(-1))])


def block_places():
    x_high, h, m = lax.axis_index("xh"), lax.axis_index("h"), lax.axis_index("m")
    count = SIZES["m"]
    zs = []
    for shift in (0, -1, 1):
        at = (m + shift + count) % count
        zs += [h * count + at, (1 - h) * count + at]
    xs = [2 * x_high + xp for xp in range(2)] + [3 - 2 * x_high - xp for xp in range(2)]
    return jnp.stack([x * SIZES["h"] * count + z for x in xs for z in zs]).astype(jnp.int32)


def product(rows, blocks):
    tensor_count, count, hidden = rows.shape
    features = blocks.shape[0] * blocks.shape[1]
    partial = lax.dot_general(
        rows.reshape(tensor_count * count, hidden),
        blocks.reshape(features, hidden),
        (((1,), (1,)), ((), ())),
        preferred_element_type=jnp.float32,
    )
    return partial.astype(jnp.bfloat16).reshape(tensor_count, count, features)


def sum_direct(partial):
    parts = lax.all_to_all(partial, "t", 0, 0)
    return jnp.sum(parts.astype(jnp.float32), axis=0).astype(jnp.bfloat16)


def sum_by_arms(low, high):
    n = low.shape[0]
    mid = n // 2
    me = lax.axis_index("t")
    up = [(i, (i + 1) % n) for i in range(n)]
    down = [(i, (i - 1) % n) for i in range(n)]
    pick = lambda value, k: lax.dynamic_index_in_dim(value, (me + k) % n, 0, keepdims=False)
    both = lambda k: jnp.concatenate([pick(low, k), pick(high, k)])
    wide = lambda value: value.astype(jnp.float32)
    narrow = lambda value: value.astype(jnp.bfloat16)

    first = lax.ppermute(pick(low, mid), "t", up)
    last = lax.ppermute(pick(high, mid), "t", down)
    going_up = jnp.concatenate([narrow(wide(pick(low, mid - 1)) + wide(first)), pick(high, mid - 1)])
    going_down = jnp.concatenate([pick(low, mid + 1), narrow(wide(pick(high, mid + 1)) + wide(last))])
    for step in range(1, mid):
        from_below = lax.ppermute(going_up, "t", up)
        from_above = lax.ppermute(going_down, "t", down)
        if step < mid - 1:
            going_up = narrow(wide(both(mid - 1 - step)) + wide(from_below))
            going_down = narrow(wide(both(mid + 1 + step)) + wide(from_above))
    return narrow(wide(both(0)) + wide(from_below) + wide(from_above))


def give_back(near, far, owners, capacity):
    features = near.shape[-1]
    rows = owners * capacity
    x_first = lax.axis_index("xp") == 0
    c_first = lax.axis_index("c") == 0
    rest = near.shape[0] // 2
    swap = lambda value: jnp.concatenate([value[rest:], value[:rest]])
    near = jnp.where(c_first, near, swap(near))
    far = jnp.where(c_first, far, swap(far))
    both = jnp.concatenate([jnp.where(x_first, near, far), jnp.where(x_first, far, near)])
    got = lax.all_to_all(both.reshape(-1, capacity, features), ("xp", "c", "e"), 0, 0)
    return got.reshape(-1, rows, features)


def place_kernel(places, onehot, *refs, width):
    out = refs[-1]
    cores = SIZES["c"]
    at = 0
    for piece in refs[:-1]:
        for xp in range(SIZES["xp"]):
            for b in range(piece.shape[2] // width):
                block = jnp.concatenate(
                    [piece[xp * cores + c, :, b * width:(b + 1) * width] for c in range(cores)], axis=1
                )
                result = jnp.dot(onehot[...], block, preferred_element_type=jnp.float32)
                start = pl.multiple_of(places[at] * (cores * width), cores * width)
                out[:, pl.ds(start, cores * width)] = result.astype(out.dtype)
                at += 1


def shards(routes, upgrad, weight):
    _, _, tensor_count, owners, capacity, hidden = upgrad.shape
    slab = weight[0]
    width = slab.shape[0]
    rows = owners * capacity

    own = upgrad.reshape(tensor_count, rows, hidden)
    column = gather_column(slab)
    x_rows = lax.ppermute(own, "xp", SWAP)
    near_rows = jnp.concatenate([own, lax.ppermute(own, "c", SWAP)], axis=1)
    far_rows = jnp.concatenate([x_rows, lax.ppermute(x_rows, "c", SWAP)], axis=1)
    other_column = lax.ppermute(column, ("xh", "xp"), WEIGHT_SWAP)

    near = sum_direct(product(near_rows, column))
    far = sum_direct(product(far_rows, column))
    summed = sum_by_arms(product(near_rows, other_column), product(far_rows, other_column))
    half = summed.shape[0] // 2
    pieces = [
        give_back(near, far, owners, capacity),
        give_back(summed[:half], summed[half:], owners, capacity),
    ]

    owner_ids = lax.iota(jnp.int32, owners)
    is_routed = jnp.any(routes[:, :, None] == owner_ids[None, None, :], axis=1)
    slot_index = jnp.cumsum(is_routed.astype(jnp.int32), axis=0) - 1
    onehot = is_routed[:, :, None] & (slot_index[:, :, None] == lax.iota(jnp.int32, capacity)[None, None, :])
    onehot = onehot.reshape(routes.shape[0], rows).astype(jnp.bfloat16)

    def body(*refs):
        place_kernel(*refs, width=width)

    smem = pl.BlockSpec(memory_space=pltpu.SMEM)
    vmem = pl.BlockSpec(memory_space=pltpu.VMEM)
    total = sum(piece.shape[0] * piece.shape[2] for piece in pieces)
    return pl.pallas_call(
        body,
        out_shape=jax.ShapeDtypeStruct((routes.shape[0], total), jnp.bfloat16),
        in_specs=[smem, vmem] + [vmem] * len(pieces),
        out_specs=vmem,
        compiler_params=pltpu.CompilerParams(vmem_limit_bytes=32 * 1024 * 1024),
    )(block_places(), onehot, *pieces)


def solution(mesh):
    fine = Mesh(mesh.devices.reshape(tuple(SIZES.values())), tuple(SIZES))
    return jax.shard_map(
        shards,
        mesh=fine,
        in_specs=(
            P(DP + ("e", "t"), None),
            P(DP, "e", None, None, None, "t"),
            P("e", DP, "t"),
        ),
        out_specs=P(DP + ("e", "t"), None),
        check_vma=False,
    )
```

```python
import jax
import jax.numpy as jnp
from jax import lax
from jax.experimental import pallas as pl
from jax.experimental.pallas import tpu as pltpu
from jax.sharding import Mesh, PartitionSpec as P

SIZES = {"xh": 2, "xp": 2, "h": 2, "m": 3, "c": 2, "e": 2, "t": 8}
DP = ("xh", "xp", "h", "m", "c")
SWAP = [(0, 1), (1, 0)]
WEIGHT_SWAP = [(i, 3 - i) for i in range(4)]


def turn(shift):
    return [(i, (i + shift) % SIZES["m"]) for i in range(SIZES["m"])]


def gather_columns(slab):
    opposite = lambda value: lax.ppermute(value, ("xh", "xp"), WEIGHT_SWAP)
    pair = jnp.stack([slab, lax.ppermute(slab, "h", SWAP)])
    rest = jnp.concatenate([lax.ppermute(pair, "m", turn(1)), lax.ppermute(pair, "m", turn(-1))])
    return jnp.concatenate([pair, rest]), opposite(pair), opposite(rest)


def block_places():
    x_high, h, m = lax.axis_index("xh"), lax.axis_index("h"), lax.axis_index("m")
    count = SIZES["m"]
    zs = []
    for shift in (0, -1, 1):
        at = (m + shift + count) % count
        zs += [h * count + at, (1 - h) * count + at]
    xs = [x for xp in range(2) for x in (2 * x_high + xp, 3 - 2 * x_high - xp)]
    return jnp.stack([x * SIZES["h"] * count + z for x in xs for z in zs]).astype(jnp.int32)


def product(rows, blocks):
    tensor_count, count, hidden = rows.shape
    features = blocks.shape[0] * blocks.shape[1]
    partial = lax.dot_general(
        rows.reshape(tensor_count * count, hidden),
        blocks.reshape(features, hidden),
        (((1,), (1,)), ((), ())),
        preferred_element_type=jnp.float32,
    )
    return partial.astype(jnp.bfloat16).reshape(tensor_count, count, features)


def sum_direct(partial):
    parts = lax.all_to_all(partial, "t", 0, 0)
    return jnp.sum(parts.astype(jnp.float32), axis=0).astype(jnp.bfloat16)


def sum_by_arms(low, high, before):
    n = low.shape[0]
    mid = n // 2
    me = lax.axis_index("t")
    up = [(i, (i + 1) % n) for i in range(n)]
    down = [(i, (i - 1) % n) for i in range(n)]
    pick = lambda value, k: lax.dynamic_index_in_dim(value, (me + k) % n, 0, keepdims=False)
    both = lambda k: jnp.concatenate([pick(low, k), pick(high, k)])
    wide = lambda value: value.astype(jnp.float32)
    narrow = lambda value: value.astype(jnp.bfloat16)

    first = lax.ppermute(pick(low, mid), "t", up)
    last = lax.ppermute(pick(high, mid), "t", down)
    going_up = jnp.concatenate([narrow(wide(pick(low, mid - 1)) + wide(first)), pick(high, mid - 1)])
    going_down = jnp.concatenate([pick(low, mid + 1), narrow(wide(pick(high, mid + 1)) + wide(last))])
    going_up, going_down, before = lax.optimization_barrier((going_up, going_down, before))
    for step in range(1, mid):
        from_below = lax.ppermute(going_up, "t", up)
        from_above = lax.ppermute(going_down, "t", down)
        if step < mid - 1:
            going_up = narrow(wide(both(mid - 1 - step)) + wide(from_below))
            going_down = narrow(wide(both(mid + 1 + step)) + wide(from_above))
    return narrow(wide(both(0)) + wide(from_below) + wide(from_above)), before


def give_back(near, far, owners, capacity):
    features = near.shape[-1]
    rows = owners * capacity
    x_first = lax.axis_index("xp") == 0
    c_first = lax.axis_index("c") == 0
    rest = near.shape[0] // 2
    swap = lambda value: jnp.concatenate([value[rest:], value[:rest]])
    near = jnp.where(c_first, near, swap(near))
    far = jnp.where(c_first, far, swap(far))
    both = jnp.concatenate([jnp.where(x_first, near, far), jnp.where(x_first, far, near)])
    got = lax.all_to_all(both.reshape(-1, capacity, features), ("xp", "c", "e"), 0, 0)
    return got.reshape(-1, rows, features)


def place_kernel(places, onehot, piece, out, *, width):
    cores = SIZES["c"]
    count = piece.shape[2] // width
    for xp in range(SIZES["xp"]):
        for b in range(count):
            block = jnp.concatenate(
                [piece[xp * cores + c, :, b * width:(b + 1) * width] for c in range(cores)], axis=1
            )
            result = jnp.dot(onehot[...], block, preferred_element_type=jnp.float32)
            start = pl.multiple_of(places[xp * count + b] * (cores * width), cores * width)
            out[:, pl.ds(start, cores * width)] = result.astype(out.dtype)


def shards(routes, upgrad, weight):
    _, _, tensor_count, owners, capacity, hidden = upgrad.shape
    slab = weight[0]
    width = slab.shape[0]
    rows = owners * capacity

    own = upgrad.reshape(tensor_count, rows, hidden)
    column, other_first, other_rest = gather_columns(slab)
    x_rows = lax.ppermute(own, "xp", SWAP)
    near_rows = jnp.concatenate([own, lax.ppermute(own, "c", SWAP)], axis=1)
    x_rows, _, other_first = lax.optimization_barrier((x_rows, column, other_first))
    far_rows = jnp.concatenate([x_rows, lax.ppermute(x_rows, "c", SWAP)], axis=1)

    near = product(near_rows, column)
    far = product(far_rows, column)
    _, _, other_first, other_rest = lax.optimization_barrier((near, far, other_first, other_rest))
    other_column = jnp.concatenate([other_first, other_rest])
    near = sum_direct(near)
    summed, near = sum_by_arms(product(near_rows, other_column), product(far_rows, other_column), near)
    far = sum_direct(far)
    half = summed.shape[0] // 2
    near = jnp.concatenate([near, summed[:half]], axis=1)
    far = jnp.concatenate([far, summed[half:]], axis=1)
    piece = give_back(near, far, owners, capacity)

    owner_ids = lax.iota(jnp.int32, owners)
    is_routed = jnp.any(routes[:, :, None] == owner_ids[None, None, :], axis=1)
    slot_index = jnp.cumsum(is_routed.astype(jnp.int32), axis=0) - 1
    onehot = is_routed[:, :, None] & (slot_index[:, :, None] == lax.iota(jnp.int32, capacity)[None, None, :])
    onehot = onehot.reshape(routes.shape[0], rows).astype(jnp.bfloat16)

    def body(*refs):
        place_kernel(*refs, width=width)

    smem = pl.BlockSpec(memory_space=pltpu.SMEM)
    vmem = pl.BlockSpec(memory_space=pltpu.VMEM)
    total = piece.shape[0] * piece.shape[2]
    return pl.pallas_call(
        body,
        out_shape=jax.ShapeDtypeStruct((routes.shape[0], total), jnp.bfloat16),
        in_specs=[smem, vmem, vmem],
        out_specs=vmem,
        compiler_params=pltpu.CompilerParams(vmem_limit_bytes=32 * 1024 * 1024),
    )(block_places(), onehot, piece)


def solution(mesh):
    fine = Mesh(mesh.devices.reshape(tuple(SIZES.values())), tuple(SIZES))
    return jax.shard_map(
        shards,
        mesh=fine,
        in_specs=(
            P(DP + ("e", "t"), None),
            P(DP, "e", None, None, None, "t"),
            P("e", DP, "t"),
        ),
        out_specs=P(DP + ("e", "t"), None),
        check_vma=False,
    )
```

```python
import jax
import jax.numpy as jnp
from jax import lax
from jax.experimental import pallas as pl
from jax.experimental.pallas import tpu as pltpu
from jax.sharding import Mesh, PartitionSpec as P

SIZES = {"xh": 2, "xp": 2, "h": 2, "m": 3, "c": 2, "e": 2, "t": 8}
DP = ("xh", "xp", "h", "m", "c")
SWAP = [(0, 1), (1, 0)]
WEIGHT_SWAP = [(i, 3 - i) for i in range(4)]


def turn(shift):
    return [(i, (i + shift) % SIZES["m"]) for i in range(SIZES["m"])]


def gather_columns(slab):
    opposite = lambda value: lax.ppermute(value, ("xh", "xp"), WEIGHT_SWAP)
    pair = jnp.stack([slab, lax.ppermute(slab, "h", SWAP)])
    rest = jnp.concatenate([lax.ppermute(pair, "m", turn(1)), lax.ppermute(pair, "m", turn(-1))])
    return (pair, rest), (opposite(pair), opposite(rest))


def block_places():
    x_high, h, m = lax.axis_index("xh"), lax.axis_index("h"), lax.axis_index("m")
    count = SIZES["m"]
    zs = []
    for shift in (0, -1, 1):
        at = (m + shift + count) % count
        zs += [h * count + at, (1 - h) * count + at]
    xs = [x for xp in range(2) for x in (2 * x_high + xp, 3 - 2 * x_high - xp)]
    return jnp.stack([x * SIZES["h"] * count + z for x in xs for z in zs]).astype(jnp.int32)


def product_kernel(place, *refs):
    (*pieces, first, rest), out = refs[:-1], refs[-1]
    step, rows, hidden = pieces[0].shape
    flat = jnp.concatenate([piece[...] for piece in pieces], axis=1).reshape(-1, hidden)
    dims = (((1,), (1,)), ((), ()))
    results = [
        lax.dot_general(flat, block[...].reshape(-1, hidden), dims, preferred_element_type=jnp.float32)
        for block in (first, rest)
    ]
    result = jnp.concatenate(results, axis=1).astype(out.dtype).reshape(out.shape)
    for k in range(len(pieces)):
        at = pl.multiple_of((place[0] ^ k) * rows, rows)
        out[:, pl.ds(at, rows), :] = result[:, k * rows:(k + 1) * rows]


def product(pieces, blocks):
    tensor_count, rows, hidden = pieces[0].shape
    rows_out = rows * len(pieces)
    features = sum(block.shape[0] * block.shape[1] for block in blocks)
    step = 2
    flops = 2 * tensor_count * rows_out * hidden * features
    moved = 2 * (tensor_count * rows_out * (hidden + features) + features * hidden)
    place = (lax.axis_index("xp") * SIZES["c"] + lax.axis_index("c")).astype(jnp.int32).reshape(1)
    return pl.pallas_call(
        product_kernel,
        grid=(tensor_count // step,),
        out_shape=jax.ShapeDtypeStruct((tensor_count, rows_out, features), jnp.bfloat16),
        in_specs=[pl.BlockSpec(memory_space=pltpu.SMEM)]
        + [pl.BlockSpec((step, rows, hidden), lambda i: (i, 0, 0))] * len(pieces)
        + [pl.BlockSpec(block.shape, lambda i: (0, 0, 0)) for block in blocks],
        out_specs=pl.BlockSpec((step, rows_out, features), lambda i: (i, 0, 0)),
        cost_estimate=pl.CostEstimate(flops=flops, bytes_accessed=moved, transcendentals=0),
        compiler_params=pltpu.CompilerParams(vmem_limit_bytes=14 * 1024 * 1024),
    )(place, *pieces, *blocks)


def sum_by_arms(partial):
    n = partial.shape[0]
    mid = n // 2
    half = partial.shape[1] // 2
    me = lax.axis_index("t")
    up = [(i, (i + 1) % n) for i in range(n)]
    down = [(i, (i - 1) % n) for i in range(n)]
    pick = lambda k: lax.dynamic_index_in_dim(partial, (me + k) % n, 0, keepdims=False)
    wide = lambda value: value.astype(jnp.float32)
    narrow = lambda value: value.astype(jnp.bfloat16)

    first = lax.ppermute(pick(mid)[:half], "t", up)
    last = lax.ppermute(pick(mid)[half:], "t", down)
    above, below = pick(mid - 1), pick(mid + 1)
    going_up = jnp.concatenate([narrow(wide(above[:half]) + wide(first)), above[half:]])
    going_down = jnp.concatenate([below[:half], narrow(wide(below[half:]) + wide(last))])
    for step in range(1, mid):
        from_below = lax.ppermute(going_up, "t", up)
        from_above = lax.ppermute(going_down, "t", down)
        if step < mid - 1:
            going_up = narrow(wide(pick(mid - 1 - step)) + wide(from_below))
            going_down = narrow(wide(pick(mid + 1 + step)) + wide(from_above))
    return narrow(wide(pick(0)) + wide(from_below) + wide(from_above))


def give_back(summed, owners, capacity):
    features = summed.shape[-1]
    got = lax.all_to_all(summed.reshape(-1, capacity, features), ("xp", "c", "e"), 0, 0)
    return got.reshape(-1, owners * capacity, features)


def place_kernel(places, onehot, piece, out, *, width):
    cores = SIZES["c"]
    count = piece.shape[2] // width
    for xp in range(SIZES["xp"]):
        for b in range(count):
            block = jnp.concatenate(
                [piece[xp * cores + c, :, b * width:(b + 1) * width] for c in range(cores)], axis=1
            )
            result = jnp.dot(onehot[...], block, preferred_element_type=jnp.float32)
            start = pl.multiple_of(places[xp * count + b] * (cores * width), cores * width)
            out[:, pl.ds(start, cores * width)] = result.astype(out.dtype)


def shards(routes, upgrad, weight):
    _, _, tensor_count, owners, capacity, hidden = upgrad.shape
    slab = weight[0]
    width = slab.shape[0]
    rows = owners * capacity

    own = upgrad.reshape(tensor_count, rows, hidden)
    column, other = gather_columns(slab)
    x_rows = lax.ppermute(own, "xp", SWAP)
    c_rows = lax.ppermute(own, "c", SWAP)
    x_rows, _, _, first = lax.optimization_barrier((x_rows, *column, other[0]))
    pieces = (own, c_rows, x_rows, lax.ppermute(x_rows, "c", SWAP))

    partial = product(pieces, column)
    partial, *other = lax.optimization_barrier((partial, first, other[1]))
    near = lax.psum_scatter(partial, "t", scatter_dimension=0, tiled=False)
    far = sum_by_arms(product(pieces, other))
    piece = give_back(jnp.concatenate([near, far], axis=1), owners, capacity)

    owner_ids = lax.iota(jnp.int32, owners)
    is_routed = jnp.any(routes[:, :, None] == owner_ids[None, None, :], axis=1)
    slot_index = jnp.cumsum(is_routed.astype(jnp.int32), axis=0) - 1
    onehot = is_routed[:, :, None] & (slot_index[:, :, None] == lax.iota(jnp.int32, capacity)[None, None, :])
    onehot = onehot.reshape(routes.shape[0], rows).astype(jnp.bfloat16)

    def body(*refs):
        place_kernel(*refs, width=width)

    smem = pl.BlockSpec(memory_space=pltpu.SMEM)
    vmem = pl.BlockSpec(memory_space=pltpu.VMEM)
    total = piece.shape[0] * piece.shape[2]
    return pl.pallas_call(
        body,
        out_shape=jax.ShapeDtypeStruct((routes.shape[0], total), jnp.bfloat16),
        in_specs=[smem, vmem, vmem],
        out_specs=vmem,
        compiler_params=pltpu.CompilerParams(vmem_limit_bytes=8 * 1024 * 1024),
    )(block_places(), onehot, piece)


def solution(mesh):
    fine = Mesh(mesh.devices.reshape(tuple(SIZES.values())), tuple(SIZES))
    return jax.shard_map(
        shards,
        mesh=fine,
        in_specs=(
            P(DP + ("e", "t"), None),
            P(DP, "e", None, None, None, "t"),
            P("e", DP, "t"),
        ),
        out_specs=P(DP + ("e", "t"), None),
        check_vma=False,
    )
```

```python
import functools

import jax
import jax.numpy as jnp
from jax import lax
from jax.experimental import pallas as pl
from jax.experimental.pallas import tpu as pltpu
from jax.sharding import Mesh, PartitionSpec as P

SIZES = {"xh": 2, "xp": 2, "h": 2, "m": 3, "c": 2, "e": 2, "t": 8}
DP = ("xh", "xp", "h", "m", "c")
SWAP = [(0, 1), (1, 0)]
WEIGHT_SWAP = [(i, 3 - i) for i in range(4)]


def turn(shift):
    return [(i, (i + shift) % SIZES["m"]) for i in range(SIZES["m"])]


def gather_columns(slab):
    opposite = lambda value: lax.ppermute(value, ("xh", "xp"), WEIGHT_SWAP)
    pair = jnp.stack([slab, lax.ppermute(slab, "h", SWAP)])
    rest = jnp.concatenate([lax.ppermute(pair, "m", turn(1)), lax.ppermute(pair, "m", turn(-1))])
    return (pair, rest), (opposite(pair), opposite(rest))


def block_places():
    x_high, h, m = lax.axis_index("xh"), lax.axis_index("h"), lax.axis_index("m")
    count = SIZES["m"]
    zs = []
    for shift in (0, -1, 1):
        at = (m + shift + count) % count
        zs += [h * count + at, (1 - h) * count + at]
    xs = [x for xp in range(2) for x in (2 * x_high + xp, 3 - 2 * x_high - xp)]
    return jnp.stack([x * SIZES["h"] * count + z for x in xs for z in zs]).astype(jnp.int32)


def product_kernel(where, *refs, pieces):
    rows, hidden = refs[0].shape[1:]
    out = refs[-1]
    flat = jnp.concatenate([piece[0] for piece in refs[:pieces]])
    dims = (((1,), (1,)), ((), ()))
    at = 0
    for block in refs[pieces:-1]:
        features = block.shape[0] * block.shape[1]
        result = lax.dot_general(
            flat, block[...].reshape(features, hidden), dims, preferred_element_type=jnp.float32
        ).astype(out.dtype)
        for k in range(pieces):
            start = pl.multiple_of((where[1] ^ k) * rows, rows)
            out[0, pl.ds(start, rows), at:at + features] = result[k * rows:(k + 1) * rows]
        at += features


def product(where, pieces, blocks, first, stride, count):
    tensor_count, rows, hidden = pieces[0].shape
    rows_out = rows * len(pieces)
    features = sum(block.shape[0] * block.shape[1] for block in blocks)
    flops = 2 * count * rows_out * hidden * features
    moved = 2 * (count * rows_out * (hidden + features) + features * hidden)

    def source(i, where):
        return ((where[0] + first + i * stride) % tensor_count, 0, 0)

    return pl.pallas_call(
        functools.partial(product_kernel, pieces=len(pieces)),
        grid_spec=pltpu.PrefetchScalarGridSpec(
            num_scalar_prefetch=1,
            grid=(count,),
            in_specs=[pl.BlockSpec((1, rows, hidden), source)] * len(pieces)
            + [pl.BlockSpec(block.shape, lambda i, where: (0, 0, 0)) for block in blocks],
            out_specs=pl.BlockSpec((1, rows_out, features), lambda i, where: (i, 0, 0)),
        ),
        out_shape=jax.ShapeDtypeStruct((count, rows_out, features), jnp.bfloat16),
        cost_estimate=pl.CostEstimate(flops=flops, bytes_accessed=moved, transcendentals=0),
        compiler_params=pltpu.CompilerParams(vmem_limit_bytes=14 * 1024 * 1024),
    )(where, *pieces, *blocks)


def sum_by_arms(partial, n):
    mid = n // 2
    up = [(i, (i + 1) % n) for i in range(n)]
    down = [(i, (i - 1) % n) for i in range(n)]
    wide = lambda value: value.astype(jnp.float32)
    narrow = lambda value: value.astype(jnp.bfloat16)

    opposite = partial(mid, 1, 1)[0]
    half = opposite.shape[0] // 2
    first = lax.ppermute(opposite[:half], "t", up)
    last = lax.ppermute(opposite[half:], "t", down)
    sides = partial(mid - 1, 2, 2)
    others = partial(mid + 2, 1, n - 3)
    above, below = sides[0], sides[1]
    going_up = jnp.concatenate([narrow(wide(above[:half]) + wide(first)), above[half:]])
    going_down = jnp.concatenate([below[:half], narrow(wide(below[half:]) + wide(last))])
    for step in range(1, mid):
        from_below = lax.ppermute(going_up, "t", up)
        from_above = lax.ppermute(going_down, "t", down)
        if step < mid - 1:
            going_up = narrow(wide(others[n - 3 - step]) + wide(from_below))
            going_down = narrow(wide(others[step - 1]) + wide(from_above))
    return narrow(wide(others[mid - 2]) + wide(from_below) + wide(from_above))


def give_back(summed, owners, capacity):
    features = summed.shape[-1]
    got = lax.all_to_all(summed.reshape(-1, capacity, features), ("xp", "c", "e"), 0, 0)
    return got.reshape(-1, owners * capacity, features)


def place_kernel(places, onehot, piece, out, *, width):
    cores = SIZES["c"]
    count = piece.shape[2] // width
    for xp in range(SIZES["xp"]):
        for b in range(count):
            block = jnp.concatenate(
                [piece[xp * cores + c, :, b * width:(b + 1) * width] for c in range(cores)], axis=1
            )
            result = jnp.dot(onehot[...], block, preferred_element_type=jnp.float32)
            start = pl.multiple_of(places[xp * count + b] * (cores * width), cores * width)
            out[:, pl.ds(start, cores * width)] = result.astype(out.dtype)


def shards(routes, upgrad, weight):
    _, _, tensor_count, owners, capacity, hidden = upgrad.shape
    slab = weight[0]
    width = slab.shape[0]
    rows = owners * capacity

    own = upgrad.reshape(tensor_count, rows, hidden)
    column, other = gather_columns(slab)
    x_rows = lax.ppermute(own, "xp", SWAP)
    c_rows = lax.ppermute(own, "c", SWAP)
    x_rows, _, _, first = lax.optimization_barrier((x_rows, *column, other[0]))
    pieces = (own, c_rows, x_rows, lax.ppermute(x_rows, "c", SWAP))

    places = [lax.axis_index("t"), lax.axis_index("xp") * SIZES["c"] + lax.axis_index("c")]
    where = jnp.stack(places).astype(jnp.int32)
    blocks = (*column, first, other[1])
    summed = sum_by_arms(
        lambda k, stride, count: product(where, pieces, blocks, k, stride, count), tensor_count
    )
    piece = give_back(summed, owners, capacity)

    owner_ids = lax.iota(jnp.int32, owners)
    is_routed = jnp.any(routes[:, :, None] == owner_ids[None, None, :], axis=1)
    slot_index = jnp.cumsum(is_routed.astype(jnp.int32), axis=0) - 1
    onehot = is_routed[:, :, None] & (slot_index[:, :, None] == lax.iota(jnp.int32, capacity)[None, None, :])
    onehot = onehot.reshape(routes.shape[0], rows).astype(jnp.bfloat16)

    def body(*refs):
        place_kernel(*refs, width=width)

    smem = pl.BlockSpec(memory_space=pltpu.SMEM)
    vmem = pl.BlockSpec(memory_space=pltpu.VMEM)
    total = piece.shape[0] * piece.shape[2]
    return pl.pallas_call(
        body,
        out_shape=jax.ShapeDtypeStruct((routes.shape[0], total), jnp.bfloat16),
        in_specs=[smem, vmem, vmem],
        out_specs=vmem,
        compiler_params=pltpu.CompilerParams(vmem_limit_bytes=8 * 1024 * 1024),
    )(block_places(), onehot, piece)


def solution(mesh):
    fine = Mesh(mesh.devices.reshape(tuple(SIZES.values())), tuple(SIZES))
    return jax.shard_map(
        shards,
        mesh=fine,
        in_specs=(
            P(DP + ("e", "t"), None),
            P(DP, "e", None, None, None, "t"),
            P("e", DP, "t"),
        ),
        out_specs=P(DP + ("e", "t"), None),
        check_vma=False,
    )
```

```python
import functools

import jax
import jax.numpy as jnp
from jax import lax
from jax.experimental import pallas as pl
from jax.experimental.pallas import tpu as pltpu
from jax.sharding import Mesh, PartitionSpec as P

SIZES = {"xh": 2, "xp": 2, "h": 2, "m": 3, "c": 2, "e": 2, "t": 8}
DP = ("xh", "xp", "h", "m", "c")
SWAP = [(0, 1), (1, 0)]
WEIGHT_SWAP = [(i, 3 - i) for i in range(4)]


def turn(shift):
    return [(i, (i + shift) % SIZES["m"]) for i in range(SIZES["m"])]


def gather_columns(slab):
    opposite = lambda value: lax.ppermute(value, ("xh", "xp"), WEIGHT_SWAP)
    pair = jnp.stack([slab, lax.ppermute(slab, "h", SWAP)])
    rest = jnp.concatenate([lax.ppermute(pair, "m", turn(1)), lax.ppermute(pair, "m", turn(-1))])
    return (pair, rest), (opposite(pair), opposite(rest))


def block_places():
    x_high, h, m = lax.axis_index("xh"), lax.axis_index("h"), lax.axis_index("m")
    count = SIZES["m"]
    zs = []
    for shift in (0, -1, 1):
        at = (m + shift + count) % count
        zs += [h * count + at, (1 - h) * count + at]
    xs = [x for xp in range(2) for x in (2 * x_high + xp, 3 - 2 * x_high - xp)]
    return jnp.stack([x * SIZES["h"] * count + z for x in xs for z in zs]).astype(jnp.int32)


def product_kernel(where, *refs, pieces):
    rows, hidden = refs[0].shape[1:]
    out = refs[-1]
    flat = jnp.concatenate([piece[0] for piece in refs[:pieces]])
    dims = (((1,), (1,)), ((), ()))
    at = 0
    for block in refs[pieces:-1]:
        features = block.shape[0] * block.shape[1]
        result = lax.dot_general(
            flat, block[...].reshape(features, hidden), dims, preferred_element_type=jnp.float32
        ).astype(out.dtype)
        for k in range(pieces):
            start = pl.multiple_of((where[1] ^ k) * rows, rows)
            out[0, pl.ds(start, rows), at:at + features] = result[k * rows:(k + 1) * rows]
        at += features


def product(where, pieces, blocks, first, stride, count):
    tensor_count, rows, hidden = pieces[0].shape
    rows_out = rows * len(pieces)
    features = sum(block.shape[0] * block.shape[1] for block in blocks)
    flops = 2 * count * rows_out * hidden * features
    moved = 2 * (count * rows_out * (hidden + features) + features * hidden)

    def source(i, where):
        return ((where[0] + first + i * stride) % tensor_count, 0, 0)

    return pl.pallas_call(
        functools.partial(product_kernel, pieces=len(pieces)),
        grid_spec=pltpu.PrefetchScalarGridSpec(
            num_scalar_prefetch=1,
            grid=(count,),
            in_specs=[pl.BlockSpec((1, rows, hidden), source)] * len(pieces)
            + [pl.BlockSpec(block.shape, lambda i, where: (0, 0, 0)) for block in blocks],
            out_specs=pl.BlockSpec((1, rows_out, features), lambda i, where: (i, 0, 0)),
        ),
        out_shape=jax.ShapeDtypeStruct((count, rows_out, features), jnp.bfloat16),
        cost_estimate=pl.CostEstimate(flops=flops, bytes_accessed=moved, transcendentals=0),
        compiler_params=pltpu.CompilerParams(vmem_limit_bytes=14 * 1024 * 1024),
    )(where, *pieces, *blocks)


def sum_by_arms(partial, n):
    mid = n // 2
    up = [(i, (i + 1) % n) for i in range(n)]
    down = [(i, (i - 1) % n) for i in range(n)]
    wide = lambda value: value.astype(jnp.float32)
    narrow = lambda value: value.astype(jnp.bfloat16)

    opposite = partial(mid, 1, 1)[0]
    half = opposite.shape[0] // 2
    first = lax.ppermute(opposite[:half], "t", up)
    last = lax.ppermute(opposite[half:], "t", down)
    above, below = partial(mid - 1, 1, 1)[0], partial(mid + 1, 1, 1)[0]
    going_up = jnp.concatenate([narrow(wide(above[:half]) + wide(first)), above[half:]])
    going_down = jnp.concatenate([below[:half], narrow(wide(below[half:]) + wide(last))])
    uppers, lowers = partial(mid - 2, -1, mid - 2), partial(mid + 2, 1, mid - 1)
    for step in range(1, mid):
        from_below = lax.ppermute(going_up, "t", up)
        from_above = lax.ppermute(going_down, "t", down)
        if step < mid - 1:
            going_up = narrow(wide(uppers[step - 1]) + wide(from_below))
            going_down = narrow(wide(lowers[step - 1]) + wide(from_above))
    return narrow(wide(lowers[mid - 2]) + wide(from_below) + wide(from_above))


def give_back(summed, capacity):
    features = summed.shape[-1]
    near = lax.all_to_all(summed.reshape(SIZES["xp"] * SIZES["c"], -1, features), ("xp", "c"), 0, 0)
    other = 1 - lax.axis_index("e")
    far = lax.ppermute(lax.dynamic_slice_in_dim(near, other * capacity, capacity, 1), "e", SWAP)
    return near, far


def place_kernel(places, near_hot, far_hot, near, far, out, *, width):
    cores = SIZES["c"]
    count = near.shape[2] // width
    for xp in range(SIZES["xp"]):
        for b in range(count):
            result = 0.0
            for hot, piece in ((near_hot, near), (far_hot, far)):
                block = jnp.concatenate(
                    [piece[xp * cores + c, :, b * width:(b + 1) * width] for c in range(cores)], axis=1
                )
                result += jnp.dot(hot[...], block, preferred_element_type=jnp.float32)
            start = pl.multiple_of(places[xp * count + b] * (cores * width), cores * width)
            out[:, pl.ds(start, cores * width)] = result.astype(out.dtype)


def shards(routes, upgrad, weight):
    _, _, tensor_count, owners, capacity, hidden = upgrad.shape
    slab = weight[0]
    width = slab.shape[0]
    rows = owners * capacity

    own = upgrad.reshape(tensor_count, rows, hidden)
    column, other = gather_columns(slab)
    x_rows = lax.ppermute(own, "xp", SWAP)
    c_rows = lax.ppermute(own, "c", SWAP)
    x_rows, _, _, first = lax.optimization_barrier((x_rows, *column, other[0]))
    pieces = (own, c_rows, x_rows, lax.ppermute(x_rows, "c", SWAP))

    places = [lax.axis_index("t"), lax.axis_index("xp") * SIZES["c"] + lax.axis_index("c")]
    where = jnp.stack(places).astype(jnp.int32)
    blocks = (*column, first, other[1])
    summed = sum_by_arms(
        lambda k, stride, count: product(where, pieces, blocks, k, stride, count), tensor_count
    )
    near, far = give_back(summed, capacity)

    me = lax.axis_index("e")
    owner_ids = jnp.stack([me, 1 - me])
    is_routed = jnp.any(routes[:, :, None] == owner_ids[None, None, :], axis=1)
    slot_index = jnp.cumsum(is_routed.astype(jnp.int32), axis=0) - 1
    near_at = jnp.where(is_routed[:, :1], slot_index[:, :1] + me * capacity, -1)
    far_at = jnp.where(is_routed[:, 1:], slot_index[:, 1:], -1)
    near_hot = (near_at == lax.iota(jnp.int32, rows)[None, :]).astype(jnp.bfloat16)
    far_hot = (far_at == lax.iota(jnp.int32, capacity)[None, :]).astype(jnp.bfloat16)

    def body(*refs):
        place_kernel(*refs, width=width)

    smem = pl.BlockSpec(memory_space=pltpu.SMEM)
    vmem = pl.BlockSpec(memory_space=pltpu.VMEM)
    total = near.shape[0] * near.shape[2]
    return pl.pallas_call(
        body,
        out_shape=jax.ShapeDtypeStruct((routes.shape[0], total), jnp.bfloat16),
        in_specs=[smem] + [vmem] * 4,
        out_specs=vmem,
        compiler_params=pltpu.CompilerParams(vmem_limit_bytes=8 * 1024 * 1024),
    )(block_places(), near_hot, far_hot, near, far)


def solution(mesh):
    fine = Mesh(mesh.devices.reshape(tuple(SIZES.values())), tuple(SIZES))
    return jax.shard_map(
        shards,
        mesh=fine,
        in_specs=(
            P(DP + ("e", "t"), None),
            P(DP, "e", None, None, None, "t"),
            P("e", DP, "t"),
        ),
        out_specs=P(DP + ("e", "t"), None),
        check_vma=False,
    )
```

```python
import functools

import jax
import jax.numpy as jnp
from jax import lax
from jax.experimental import pallas as pl
from jax.experimental.pallas import tpu as pltpu
from jax.sharding import Mesh, PartitionSpec as P

SIZES = {"xh": 2, "xp": 2, "h": 2, "m": 3, "c": 2, "e": 2, "t": 8}
DP = ("xh", "xp", "h", "m", "c")
SWAP = [(0, 1), (1, 0)]
WEIGHT_SWAP = [(i, 3 - i) for i in range(4)]


def turn(shift):
    return [(i, (i + shift) % SIZES["m"]) for i in range(SIZES["m"])]


def gather_columns(slab):
    opposite = lambda value: lax.ppermute(value, ("xh", "xp"), WEIGHT_SWAP)
    pair = jnp.stack([slab, lax.ppermute(slab, "h", SWAP)])
    blocks = (pair, lax.ppermute(pair, "m", turn(1)), lax.ppermute(pair, "m", turn(-1)))
    return blocks, [opposite(block) for block in blocks]


def block_places():
    x_high, h, m = lax.axis_index("xh"), lax.axis_index("h"), lax.axis_index("m")
    count = SIZES["m"]
    zs = []
    for shift in (0, -1, 1):
        at = (m + shift + count) % count
        zs += [h * count + at, (1 - h) * count + at]
    xs = [x for xp in range(2) for x in (2 * x_high + xp, 3 - 2 * x_high - xp)]
    return jnp.stack([x * SIZES["h"] * count + z for x in xs for z in zs]).astype(jnp.int32)


def product_kernel(where, *refs, pieces, outs):
    rows, hidden = refs[0].shape[1:]
    flat = jnp.concatenate([piece[0] for piece in refs[:pieces]])
    weights = jnp.concatenate([block[...].reshape(-1, hidden) for block in refs[pieces:-outs]])
    result = lax.dot_general(
        flat, weights, (((1,), (1,)), ((), ())), preferred_element_type=jnp.float32
    ).astype(jnp.bfloat16)
    for i, out in enumerate(refs[-outs:]):

        @pl.when(pl.program_id(0) == i)
        def _():
            for k in range(pieces):
                start = pl.multiple_of((where[1] ^ k) * rows, rows)
                out[pl.ds(start, rows), :] = result[k * rows:(k + 1) * rows]


def product(where, pieces, blocks, first, stride, count):
    tensor_count, rows, hidden = pieces[0].shape
    rows_out = rows * len(pieces)
    features = sum(block.shape[0] * block.shape[1] for block in blocks)
    flops = 2 * count * rows_out * hidden * features
    moved = 2 * (count * rows_out * (hidden + features) + features * hidden)

    def source(i, where):
        return ((where[0] + first + i * stride) % tensor_count, 0, 0)

    return pl.pallas_call(
        functools.partial(product_kernel, pieces=len(pieces), outs=count),
        grid_spec=pltpu.PrefetchScalarGridSpec(
            num_scalar_prefetch=1,
            grid=(count,),
            in_specs=[pl.BlockSpec((1, rows, hidden), source)] * len(pieces)
            + [pl.BlockSpec(block.shape, lambda i, where: (0, 0, 0)) for block in blocks],
            out_specs=[pl.BlockSpec((rows_out, features), lambda i, where: (0, 0))] * count,
        ),
        out_shape=[jax.ShapeDtypeStruct((rows_out, features), jnp.bfloat16)] * count,
        cost_estimate=pl.CostEstimate(flops=flops, bytes_accessed=moved, transcendentals=0),
        compiler_params=pltpu.CompilerParams(vmem_limit_bytes=20 * 1024 * 1024),
    )(where, *pieces, *blocks)


def sum_by_arms(partial, n):
    mid = n // 2
    up = [(i, (i + 1) % n) for i in range(n)]
    down = [(i, (i - 1) % n) for i in range(n)]
    wide = lambda value: value.astype(jnp.float32)
    narrow = lambda value: value.astype(jnp.bfloat16)

    (opposite,) = partial(mid, 1, 1)
    half = opposite.shape[0] // 2
    first = lax.ppermute(opposite[:half], "t", up)
    last = lax.ppermute(opposite[half:], "t", down)
    above, below = partial(mid - 1, 2, 2)
    going_up = jnp.concatenate([narrow(wide(above[:half]) + wide(first)), above[half:]])
    going_down = jnp.concatenate([below[:half], narrow(wide(below[half:]) + wide(last))])
    others = partial(mid + 2, 1, n - 3)
    lowers, uppers = others[:mid - 1], others[:mid - 2:-1]
    for step in range(1, mid):
        from_below = lax.ppermute(going_up, "t", up)
        from_above = lax.ppermute(going_down, "t", down)
        if step < mid - 1:
            going_up = narrow(wide(uppers[step - 1]) + wide(from_below))
            going_down = narrow(wide(lowers[step - 1]) + wide(from_above))
    return narrow(wide(lowers[mid - 2]) + wide(from_below) + wide(from_above))


def give_back(summed, owners, capacity):
    features = summed.shape[-1]
    got = lax.all_to_all(summed.reshape(-1, capacity, features), ("xp", "c", "e"), 0, 0)
    return got.reshape(-1, owners * capacity, features)


def place_kernel(places, onehot, piece, out, *, width):
    cores = SIZES["c"]
    count = piece.shape[2] // width
    for xp in range(SIZES["xp"]):
        for b in range(count):
            block = jnp.concatenate(
                [piece[xp * cores + c, :, b * width:(b + 1) * width] for c in range(cores)], axis=1
            )
            result = jnp.dot(onehot[...], block, preferred_element_type=jnp.float32)
            start = pl.multiple_of(places[xp * count + b] * (cores * width), cores * width)
            out[:, pl.ds(start, cores * width)] = result.astype(out.dtype)


def shards(routes, upgrad, weight):
    _, _, tensor_count, owners, capacity, hidden = upgrad.shape
    slab = weight[0]
    width = slab.shape[0]
    rows = owners * capacity

    own = upgrad.reshape(tensor_count, rows, hidden)
    column, other = gather_columns(slab)
    x_rows = lax.ppermute(own, "xp", SWAP)
    c_rows = lax.ppermute(own, "c", SWAP)
    x_rows, *_ = lax.optimization_barrier((x_rows, *column, *other[:2]))
    pieces = (own, c_rows, x_rows, lax.ppermute(x_rows, "c", SWAP))

    places = [lax.axis_index("t"), lax.axis_index("xp") * SIZES["c"] + lax.axis_index("c")]
    where = jnp.stack(places).astype(jnp.int32)
    blocks = (*column, *other)
    summed = sum_by_arms(
        lambda k, stride, count: product(where, pieces, blocks, k, stride, count), tensor_count
    )
    piece = give_back(summed, owners, capacity)

    owner_ids = lax.iota(jnp.int32, owners)
    is_routed = jnp.any(routes[:, :, None] == owner_ids[None, None, :], axis=1)
    slot_index = jnp.cumsum(is_routed.astype(jnp.int32), axis=0) - 1
    onehot = is_routed[:, :, None] & (slot_index[:, :, None] == lax.iota(jnp.int32, capacity)[None, None, :])
    onehot = onehot.reshape(routes.shape[0], rows).astype(jnp.bfloat16)

    def body(*refs):
        place_kernel(*refs, width=width)

    smem = pl.BlockSpec(memory_space=pltpu.SMEM)
    vmem = pl.BlockSpec(memory_space=pltpu.VMEM)
    total = piece.shape[0] * piece.shape[2]
    return pl.pallas_call(
        body,
        out_shape=jax.ShapeDtypeStruct((routes.shape[0], total), jnp.bfloat16),
        in_specs=[smem, vmem, vmem],
        out_specs=vmem,
        compiler_params=pltpu.CompilerParams(vmem_limit_bytes=8 * 1024 * 1024),
    )(block_places(), onehot, piece)


def solution(mesh):
    fine = Mesh(mesh.devices.reshape(tuple(SIZES.values())), tuple(SIZES))
    return jax.shard_map(
        shards,
        mesh=fine,
        in_specs=(
            P(DP + ("e", "t"), None),
            P(DP, "e", None, None, None, "t"),
            P("e", DP, "t"),
        ),
        out_specs=P(DP + ("e", "t"), None),
        check_vma=False,
    )
```

```python
import functools

import jax
import jax.numpy as jnp
from jax import lax
from jax.experimental import pallas as pl
from jax.experimental.pallas import tpu as pltpu
from jax.sharding import Mesh, PartitionSpec as P

SIZES = {"xh": 2, "xp": 2, "h": 2, "m": 3, "c": 2, "e": 2, "t": 8}
DP = ("xh", "xp", "h", "m", "c")
SWAP = [(0, 1), (1, 0)]
WEIGHT_SWAP = [(i, 3 - i) for i in range(4)]


def turn(shift):
    return [(i, (i + shift) % SIZES["m"]) for i in range(SIZES["m"])]


def gather_columns(slab, before):
    opposite = lambda value: lax.ppermute(value, ("xh", "xp"), WEIGHT_SWAP)
    pair, before = lax.optimization_barrier((jnp.stack([slab, lax.ppermute(slab, "h", SWAP)]), before))
    blocks = (pair, lax.ppermute(pair, "m", turn(1)), lax.ppermute(pair, "m", turn(-1)))
    return blocks, [opposite(block) for block in blocks], before


def block_places():
    x_high, h, m = lax.axis_index("xh"), lax.axis_index("h"), lax.axis_index("m")
    count = SIZES["m"]
    zs = []
    for shift in (0, -1, 1):
        at = (m + shift + count) % count
        zs += [h * count + at, (1 - h) * count + at]
    xs = [x for xp in range(2) for x in (2 * x_high + xp, 3 - 2 * x_high - xp)]
    return jnp.stack([x * SIZES["h"] * count + z for x in xs for z in zs]).astype(jnp.int32)


def product_kernel(where, *refs, pieces, outs):
    rows, hidden = refs[0].shape[1:]
    flat = jnp.concatenate([piece[0] for piece in refs[:pieces]])
    weights = jnp.concatenate([block[...].reshape(-1, hidden) for block in refs[pieces:-outs]])
    result = lax.dot_general(
        flat, weights, (((1,), (1,)), ((), ())), preferred_element_type=jnp.float32
    ).astype(jnp.bfloat16)
    for i, out in enumerate(refs[-outs:]):

        @pl.when(pl.program_id(0) == i)
        def _():
            for k in range(pieces):
                start = pl.multiple_of((where[1] ^ k) * rows, rows)
                out[pl.ds(start, rows), :] = result[k * rows:(k + 1) * rows]


def product(where, pieces, blocks, first, stride, count):
    tensor_count, rows, hidden = pieces[0].shape
    rows_out = rows * len(pieces)
    features = sum(block.shape[0] * block.shape[1] for block in blocks)
    flops = 2 * count * rows_out * hidden * features
    moved = 2 * (count * rows_out * (hidden + features) + features * hidden)

    def source(i, where):
        return ((where[0] + first + i * stride) % tensor_count, 0, 0)

    return pl.pallas_call(
        functools.partial(product_kernel, pieces=len(pieces), outs=count),
        grid_spec=pltpu.PrefetchScalarGridSpec(
            num_scalar_prefetch=1,
            grid=(count,),
            in_specs=[pl.BlockSpec((1, rows, hidden), source)] * len(pieces)
            + [pl.BlockSpec(block.shape, lambda i, where: (0, 0, 0)) for block in blocks],
            out_specs=[pl.BlockSpec((rows_out, features), lambda i, where: (0, 0))] * count,
        ),
        out_shape=[jax.ShapeDtypeStruct((rows_out, features), jnp.bfloat16)] * count,
        cost_estimate=pl.CostEstimate(flops=flops, bytes_accessed=moved, transcendentals=0),
        compiler_params=pltpu.CompilerParams(vmem_limit_bytes=56 * 1024 * 1024),
    )(where, *pieces, *blocks)


def sum_by_arms(partial, n):
    mid = n // 2
    up = [(i, (i + 1) % n) for i in range(n)]
    down = [(i, (i - 1) % n) for i in range(n)]
    wide = lambda value: value.astype(jnp.float32)
    narrow = lambda value: value.astype(jnp.bfloat16)

    (opposite,) = partial(mid, 1, 1)
    half = opposite.shape[0] // 2
    first = lax.ppermute(opposite[:half], "t", up)
    last = lax.ppermute(opposite[half:], "t", down)
    above, below = partial(mid - 1, 2, 2)
    going_up = jnp.concatenate([narrow(wide(above[:half]) + wide(first)), above[half:]])
    going_down = jnp.concatenate([below[:half], narrow(wide(below[half:]) + wide(last))])
    others = partial(mid + 2, 1, n - 3)
    lowers, uppers = others[:mid - 1], others[:mid - 2:-1]
    for step in range(1, mid):
        from_below = lax.ppermute(going_up, "t", up)
        from_above = lax.ppermute(going_down, "t", down)
        if step < mid - 1:
            going_up = narrow(wide(uppers[step - 1]) + wide(from_below))
            going_down = narrow(wide(lowers[step - 1]) + wide(from_above))
    return narrow(wide(lowers[mid - 2]) + wide(from_below) + wide(from_above))


def give_back(summed, owners, capacity):
    features = summed.shape[-1]
    got = lax.all_to_all(summed.reshape(-1, capacity, features), ("xp", "c", "e"), 0, 0)
    return got.reshape(-1, owners * capacity, features)


def place_kernel(places, onehot, piece, out, *, width):
    cores = SIZES["c"]
    count = piece.shape[2] // width
    for xp in range(SIZES["xp"]):
        for b in range(count):
            block = jnp.concatenate(
                [piece[xp * cores + c, :, b * width:(b + 1) * width] for c in range(cores)], axis=1
            )
            result = jnp.dot(onehot[...], block, preferred_element_type=jnp.float32)
            start = pl.multiple_of(places[xp * count + b] * (cores * width), cores * width)
            out[:, pl.ds(start, cores * width)] = result.astype(out.dtype)


def shards(routes, upgrad, weight):
    _, _, tensor_count, owners, capacity, hidden = upgrad.shape
    slab = weight[0]
    width = slab.shape[0]
    rows = owners * capacity

    own = upgrad.reshape(tensor_count, rows, hidden)
    x_rows = lax.ppermute(own, "xp", SWAP)
    column, other, c_rows = gather_columns(slab, lax.ppermute(own, "c", SWAP))
    x_rows, *_ = lax.optimization_barrier((x_rows, *column, *other))
    pieces = (own, c_rows, x_rows, lax.ppermute(x_rows, "c", SWAP))

    places = [lax.axis_index("t"), lax.axis_index("xp") * SIZES["c"] + lax.axis_index("c")]
    where = jnp.stack(places).astype(jnp.int32)
    blocks = (*column, *other)
    summed = sum_by_arms(
        lambda k, stride, count: product(where, pieces, blocks, k, stride, count), tensor_count
    )
    piece = give_back(summed, owners, capacity)

    owner_ids = lax.iota(jnp.int32, owners)
    is_routed = jnp.any(routes[:, :, None] == owner_ids[None, None, :], axis=1)
    slot_index = jnp.cumsum(is_routed.astype(jnp.int32), axis=0) - 1
    onehot = is_routed[:, :, None] & (slot_index[:, :, None] == lax.iota(jnp.int32, capacity)[None, None, :])
    onehot = onehot.reshape(routes.shape[0], rows).astype(jnp.bfloat16)

    def body(*refs):
        place_kernel(*refs, width=width)

    smem = pl.BlockSpec(memory_space=pltpu.SMEM)
    vmem = pl.BlockSpec(memory_space=pltpu.VMEM)
    total = piece.shape[0] * piece.shape[2]
    return pl.pallas_call(
        body,
        out_shape=jax.ShapeDtypeStruct((routes.shape[0], total), jnp.bfloat16),
        in_specs=[smem, vmem, vmem],
        out_specs=vmem,
        compiler_params=pltpu.CompilerParams(vmem_limit_bytes=8 * 1024 * 1024),
    )(block_places(), onehot, piece)


def solution(mesh):
    fine = Mesh(mesh.devices.reshape(tuple(SIZES.values())), tuple(SIZES))
    return jax.shard_map(
        shards,
        mesh=fine,
        in_specs=(
            P(DP + ("e", "t"), None),
            P(DP, "e", None, None, None, "t"),
            P("e", DP, "t"),
        ),
        out_specs=P(DP + ("e", "t"), None),
        check_vma=False,
    )
```

```python
import functools

import jax
import jax.numpy as jnp
from jax import lax
from jax.experimental import pallas as pl
from jax.experimental.pallas import tpu as pltpu
from jax.sharding import Mesh, PartitionSpec as P

SIZES = {"xh": 2, "xp": 2, "h": 2, "m": 3, "c": 2, "e": 2, "t": 8}
DP = ("xh", "xp", "h", "m", "c")
SWAP = [(0, 1), (1, 0)]
WEIGHT_SWAP = [(i, 3 - i) for i in range(4)]


def turn(shift):
    return [(i, (i + shift) % SIZES["m"]) for i in range(SIZES["m"])]


def gather_columns(slab):
    opposite = lambda value: lax.ppermute(value, ("xh", "xp"), WEIGHT_SWAP)
    pair = jnp.stack([slab, lax.ppermute(slab, "h", SWAP)])
    blocks = (pair, lax.ppermute(pair, "m", turn(1)), lax.ppermute(pair, "m", turn(-1)))
    return blocks, [opposite(block) for block in blocks]


def block_places():
    x_high, h, m = lax.axis_index("xh"), lax.axis_index("h"), lax.axis_index("m")
    count = SIZES["m"]
    zs = []
    for shift in (0, -1, 1):
        at = (m + shift + count) % count
        zs += [h * count + at, (1 - h) * count + at]
    xs = [x for xp in range(2) for x in (2 * x_high + xp, 3 - 2 * x_high - xp)]
    return jnp.stack([x * SIZES["h"] * count + z for x in xs for z in zs]).astype(jnp.int32)


def product_kernel(here, place, *refs, pieces, outs):
    rows, hidden = refs[0].shape[1:]
    flat = jnp.concatenate([piece[0] for piece in refs[:pieces]])
    weights = jnp.concatenate([block[...].reshape(-1, hidden) for block in refs[pieces:-outs]])
    result = lax.dot_general(
        flat, weights, (((1,), (1,)), ((), ())), preferred_element_type=jnp.float32
    ).astype(jnp.bfloat16)
    for i, out in enumerate(refs[-outs:]):

        @pl.when(pl.program_id(0) == i)
        def _():
            for k in range(pieces):
                start = pl.multiple_of((place[0] ^ k) * rows, rows)
                out[pl.ds(start, rows), :] = result[k * rows:(k + 1) * rows]


def product(where, pieces, blocks, first, stride, count):
    tensor_count, rows, hidden = pieces[0].shape
    rows_out = rows * len(pieces)
    features = sum(block.shape[0] * block.shape[1] for block in blocks)
    flops = 2 * count * rows_out * hidden * features
    moved = 2 * (count * rows_out * (hidden + features) + features * hidden)

    def source(i, here, place):
        return ((here[0] + first + i * stride) % tensor_count, 0, 0)

    return pl.pallas_call(
        functools.partial(product_kernel, pieces=len(pieces), outs=count),
        grid_spec=pltpu.PrefetchScalarGridSpec(
            num_scalar_prefetch=2,
            grid=(count,),
            in_specs=[pl.BlockSpec((1, rows, hidden), source)] * len(pieces)
            + [pl.BlockSpec(block.shape, lambda i, here, place: (0, 0, 0)) for block in blocks],
            out_specs=[pl.BlockSpec((rows_out, features), lambda i, here, place: (0, 0))] * count,
        ),
        out_shape=[jax.ShapeDtypeStruct((rows_out, features), jnp.bfloat16)] * count,
        cost_estimate=pl.CostEstimate(flops=flops, bytes_accessed=moved, transcendentals=0),
        compiler_params=pltpu.CompilerParams(vmem_limit_bytes=14 * 1024 * 1024),
    )(*where, *pieces, *blocks)


def sum_by_arms(partial, n):
    mid = n // 2
    up = [(i, (i + 1) % n) for i in range(n)]
    down = [(i, (i - 1) % n) for i in range(n)]
    wide = lambda value: value.astype(jnp.float32)
    narrow = lambda value: value.astype(jnp.bfloat16)

    (opposite,) = partial(mid, 1, 1)
    half = opposite.shape[0] // 2
    first = lax.ppermute(opposite[:half], "t", up)
    last = lax.ppermute(opposite[half:], "t", down)
    above, below = partial(mid - 1, 2, 2)
    going_up = jnp.concatenate([narrow(wide(above[:half]) + wide(first)), above[half:]])
    going_down = jnp.concatenate([below[:half], narrow(wide(below[half:]) + wide(last))])
    uppers, lowers = partial(mid - 2, -1, mid - 2), partial(mid + 2, 1, mid - 1)
    for step in range(1, mid):
        from_below = lax.ppermute(going_up, "t", up)
        from_above = lax.ppermute(going_down, "t", down)
        if step < mid - 1:
            going_up = narrow(wide(uppers[step - 1]) + wide(from_below))
            going_down = narrow(wide(lowers[step - 1]) + wide(from_above))
    return narrow(wide(lowers[mid - 2]) + wide(from_below) + wide(from_above))


def give_back(summed, owners, capacity):
    features = summed.shape[-1]
    got = lax.all_to_all(summed.reshape(-1, capacity, features), ("xp", "c", "e"), 0, 0)
    return got.reshape(-1, owners * capacity, features)


def place_kernel(places, onehot, piece, out, *, width):
    cores = SIZES["c"]
    count = piece.shape[2] // width
    for xp in range(SIZES["xp"]):
        for b in range(count):
            block = jnp.concatenate(
                [piece[xp * cores + c, :, b * width:(b + 1) * width] for c in range(cores)], axis=1
            )
            result = jnp.dot(onehot[...], block, preferred_element_type=jnp.float32)
            start = pl.multiple_of(places[xp * count + b] * (cores * width), cores * width)
            out[:, pl.ds(start, cores * width)] = result.astype(out.dtype)


def shards(routes, upgrad, weight):
    _, _, tensor_count, owners, capacity, hidden = upgrad.shape
    slab = weight[0]
    width = slab.shape[0]
    rows = owners * capacity

    own = upgrad.reshape(tensor_count, rows, hidden)
    x_rows = lax.ppermute(own, "xp", SWAP)
    c_rows = lax.ppermute(own, "c", SWAP)
    column, other = gather_columns(slab)
    x_rows, *_ = lax.optimization_barrier((x_rows, *column, *other))
    pieces = (own, c_rows, x_rows, lax.ppermute(x_rows, "c", SWAP))

    places = [lax.axis_index("t"), lax.axis_index("xp") * SIZES["c"] + lax.axis_index("c")]
    where = [place.astype(jnp.int32).reshape(1) for place in places]
    blocks = (*column, *other)
    summed = sum_by_arms(
        lambda k, stride, count: product(where, pieces, blocks, k, stride, count), tensor_count
    )
    piece = give_back(summed, owners, capacity)

    owner_ids = lax.iota(jnp.int32, owners)
    is_routed = jnp.any(routes[:, :, None] == owner_ids[None, None, :], axis=1)
    slot_index = jnp.cumsum(is_routed.astype(jnp.int32), axis=0) - 1
    onehot = is_routed[:, :, None] & (slot_index[:, :, None] == lax.iota(jnp.int32, capacity)[None, None, :])
    onehot = onehot.reshape(routes.shape[0], rows).astype(jnp.bfloat16)

    def body(*refs):
        place_kernel(*refs, width=width)

    smem = pl.BlockSpec(memory_space=pltpu.SMEM)
    vmem = pl.BlockSpec(memory_space=pltpu.VMEM)
    total = piece.shape[0] * piece.shape[2]
    return pl.pallas_call(
        body,
        out_shape=jax.ShapeDtypeStruct((routes.shape[0], total), jnp.bfloat16),
        in_specs=[smem, vmem, vmem],
        out_specs=vmem,
        compiler_params=pltpu.CompilerParams(vmem_limit_bytes=8 * 1024 * 1024),
    )(block_places(), onehot, piece)


def solution(mesh):
    fine = Mesh(mesh.devices.reshape(tuple(SIZES.values())), tuple(SIZES))
    return jax.shard_map(
        shards,
        mesh=fine,
        in_specs=(
            P(DP + ("e", "t"), None),
            P(DP, "e", None, None, None, "t"),
            P("e", DP, "t"),
        ),
        out_specs=P(DP + ("e", "t"), None),
        check_vma=False,
    )
```

```python
import functools

import jax
import jax.numpy as jnp
from jax import lax
from jax.experimental import pallas as pl
from jax.experimental.pallas import tpu as pltpu
from jax.sharding import Mesh, PartitionSpec as P

SIZES = {"xh": 2, "xp": 2, "h": 2, "m": 3, "c": 2, "e": 2, "t": 8}
DP = ("xh", "xp", "h", "m", "c")
SWAP = [(0, 1), (1, 0)]
WEIGHT_SWAP = [(i, 3 - i) for i in range(4)]


def turn(shift):
    return [(i, (i + shift) % SIZES["m"]) for i in range(SIZES["m"])]


def gather_columns(slab):
    opposite = lambda value: lax.ppermute(value, ("xh", "xp"), WEIGHT_SWAP)
    pair = jnp.stack([slab, lax.ppermute(slab, "h", SWAP)])
    blocks = (pair, lax.ppermute(pair, "m", turn(1)), lax.ppermute(pair, "m", turn(-1)))
    return blocks, [opposite(block) for block in blocks]


def block_places():
    x_high, h, m = lax.axis_index("xh"), lax.axis_index("h"), lax.axis_index("m")
    count = SIZES["m"]
    zs = []
    for shift in (0, -1, 1):
        at = (m + shift + count) % count
        zs += [h * count + at, (1 - h) * count + at]
    xs = [x for xp in range(2) for x in (2 * x_high + xp, 3 - 2 * x_high - xp)]
    return jnp.stack([x * SIZES["h"] * count + z for x in xs for z in zs]).astype(jnp.int32)


def product_kernel(here, place, *refs, pieces, outs):
    rows, hidden = refs[0].shape[1:]
    flat = jnp.concatenate([piece[0] for piece in refs[:pieces]])
    blocks = refs[pieces:-outs[0] * outs[1]]
    weights = jnp.concatenate([block[...].reshape(-1, hidden) for block in blocks])
    result = lax.dot_general(
        flat, weights, (((1,), (1,)), ((), ())), preferred_element_type=jnp.float32
    ).astype(jnp.bfloat16)
    rest = [result[k * rows:(k + 1) * rows] for k in range(pieces)]
    step = 1
    while step < pieces:
        flip = (place[0] // step) % 2 == 1
        rest = [jnp.where(flip, rest[k ^ step], rest[k]) for k in range(pieces)]
        step *= 2
    share = pieces if outs[0] > 1 else pieces // outs[1]
    for i, out in enumerate(refs[-outs[0] * outs[1]:]):
        part = i % outs[1]

        @pl.when(pl.program_id(0) == i // outs[1])
        def _():
            for k in range(share):
                out[k * rows:(k + 1) * rows, :] = rest[part * share + k]


def product(where, pieces, blocks, first, stride, count, parts=1):
    tensor_count, rows, hidden = pieces[0].shape
    rows_out = rows * len(pieces)
    outs = count * parts
    features = sum(block.shape[0] * block.shape[1] for block in blocks)
    flops = 2 * count * rows_out * hidden * features
    moved = 2 * (count * rows_out * (hidden + features) + features * hidden)

    def source(i, here, place):
        return ((here[0] + first + i * stride) % tensor_count, 0, 0)

    return pl.pallas_call(
        functools.partial(product_kernel, pieces=len(pieces), outs=(count, parts)),
        grid_spec=pltpu.PrefetchScalarGridSpec(
            num_scalar_prefetch=2,
            grid=(count,),
            in_specs=[pl.BlockSpec((1, rows, hidden), source)] * len(pieces)
            + [pl.BlockSpec(block.shape, lambda i, here, place: (0, 0, 0)) for block in blocks],
            out_specs=[pl.BlockSpec((rows_out // parts, features), lambda i, here, place: (0, 0))] * outs,
        ),
        out_shape=[jax.ShapeDtypeStruct((rows_out // parts, features), jnp.bfloat16)] * outs,
        cost_estimate=pl.CostEstimate(flops=flops, bytes_accessed=moved, transcendentals=0),
        compiler_params=pltpu.CompilerParams(vmem_limit_bytes=14 * 1024 * 1024),
    )(*where, *pieces, *blocks)


def add_kernel(*refs, at):
    *terms, out = refs
    base, came = terms[0], terms[1:]
    rows = came[0].shape[0]
    total = base[at:at + rows, :].astype(jnp.float32)
    for term in came:
        total += term[...].astype(jnp.float32)
    out[at:at + rows, :] = total.astype(out.dtype)
    for low, high in ((0, at), (at + rows, base.shape[0])):
        if low < high:
            out[low:high, :] = base[low:high, :]


def add(base, *came, at=0):
    vmem = pl.BlockSpec(memory_space=pltpu.VMEM)
    size = base.size
    return pl.pallas_call(
        functools.partial(add_kernel, at=at),
        out_shape=jax.ShapeDtypeStruct(base.shape, base.dtype),
        in_specs=[vmem] * (1 + len(came)),
        out_specs=vmem,
        cost_estimate=pl.CostEstimate(flops=size, bytes_accessed=6 * size, transcendentals=0),
        compiler_params=pltpu.CompilerParams(vmem_limit_bytes=8 * 1024 * 1024),
    )(base, *came)


def sum_by_arms(partial, n):
    mid = n // 2
    up = [(i, (i + 1) % n) for i in range(n)]
    down = [(i, (i - 1) % n) for i in range(n)]

    low, high = partial(mid, 1, 1, 2)
    first = lax.ppermute(low, "t", up)
    last = lax.ppermute(high, "t", down)
    above, below = partial(mid - 1, 2, 2, 1)
    going_up = add(above, first)
    going_down = add(below, last, at=low.shape[0])
    uppers, lowers = partial(mid - 2, -1, mid - 2, 1), partial(mid + 2, 1, mid - 1, 1)
    for step in range(1, mid):
        from_below = lax.ppermute(going_up, "t", up)
        from_above = lax.ppermute(going_down, "t", down)
        if step < mid - 1:
            going_up = add(uppers[step - 1], from_below)
            going_down = add(lowers[step - 1], from_above)
    return add(lowers[mid - 2], from_below, from_above)


def give_back(summed, owners, capacity):
    features = summed.shape[-1]
    got = lax.all_to_all(summed.reshape(-1, capacity, features), ("xp", "c", "e"), 0, 0)
    return got.reshape(-1, owners * capacity, features)


def place_kernel(places, onehot, piece, out, *, width):
    cores = SIZES["c"]
    count = piece.shape[2] // width
    for xp in range(SIZES["xp"]):
        for b in range(count):
            block = jnp.concatenate(
                [piece[xp * cores + c, :, b * width:(b + 1) * width] for c in range(cores)], axis=1
            )
            result = jnp.dot(onehot[...], block, preferred_element_type=jnp.float32)
            start = pl.multiple_of(places[xp * count + b] * (cores * width), cores * width)
            out[:, pl.ds(start, cores * width)] = result.astype(out.dtype)


def shards(routes, upgrad, weight):
    _, _, tensor_count, owners, capacity, hidden = upgrad.shape
    slab = weight[0]
    width = slab.shape[0]
    rows = owners * capacity

    own = upgrad.reshape(tensor_count, rows, hidden)
    x_rows = lax.ppermute(own, "xp", SWAP)
    c_rows = lax.ppermute(own, "c", SWAP)
    column, other = gather_columns(slab)
    x_rows, *_ = lax.optimization_barrier((x_rows, *column, *other))
    pieces = (own, c_rows, x_rows, lax.ppermute(x_rows, "c", SWAP))

    places = [lax.axis_index("t"), lax.axis_index("xp") * SIZES["c"] + lax.axis_index("c")]
    where = [place.astype(jnp.int32).reshape(1) for place in places]
    blocks = (*column, *other)
    summed = sum_by_arms(
        lambda *at: product(where, pieces, blocks, *at), tensor_count
    )
    piece = give_back(summed, owners, capacity)

    owner_ids = lax.iota(jnp.int32, owners)
    is_routed = jnp.any(routes[:, :, None] == owner_ids[None, None, :], axis=1)
    slot_index = jnp.cumsum(is_routed.astype(jnp.int32), axis=0) - 1
    onehot = is_routed[:, :, None] & (slot_index[:, :, None] == lax.iota(jnp.int32, capacity)[None, None, :])
    onehot = onehot.reshape(routes.shape[0], rows).astype(jnp.bfloat16)

    def body(*refs):
        place_kernel(*refs, width=width)

    smem = pl.BlockSpec(memory_space=pltpu.SMEM)
    vmem = pl.BlockSpec(memory_space=pltpu.VMEM)
    total = piece.shape[0] * piece.shape[2]
    return pl.pallas_call(
        body,
        out_shape=jax.ShapeDtypeStruct((routes.shape[0], total), jnp.bfloat16),
        in_specs=[smem, vmem, vmem],
        out_specs=vmem,
        compiler_params=pltpu.CompilerParams(vmem_limit_bytes=8 * 1024 * 1024),
    )(block_places(), onehot, piece)


def solution(mesh):
    fine = Mesh(mesh.devices.reshape(tuple(SIZES.values())), tuple(SIZES))
    return jax.shard_map(
        shards,
        mesh=fine,
        in_specs=(
            P(DP + ("e", "t"), None),
            P(DP, "e", None, None, None, "t"),
            P("e", DP, "t"),
        ),
        out_specs=P(DP + ("e", "t"), None),
        check_vma=False,
    )
```

```python
import functools

import jax
import jax.numpy as jnp
from jax import lax
from jax.experimental import pallas as pl
from jax.experimental.pallas import tpu as pltpu
from jax.sharding import Mesh, PartitionSpec as P

SIZES = {"xh": 2, "xp": 2, "h": 2, "m": 3, "c": 2, "e": 2, "t": 8}
DP = ("xh", "xp", "h", "m", "c")
SWAP = [(0, 1), (1, 0)]
WEIGHT_SWAP = [(i, 3 - i) for i in range(4)]


def turn(shift):
    return [(i, (i + shift) % SIZES["m"]) for i in range(SIZES["m"])]


def gather_columns(slab):
    opposite = lambda value: lax.ppermute(value, ("xh", "xp"), WEIGHT_SWAP)
    pair = jnp.stack([slab, lax.ppermute(slab, "h", SWAP)])
    blocks = (pair, lax.ppermute(pair, "m", turn(1)), lax.ppermute(pair, "m", turn(-1)))
    return blocks, [opposite(block) for block in blocks]


def block_places():
    x_high, h, m = lax.axis_index("xh"), lax.axis_index("h"), lax.axis_index("m")
    count = SIZES["m"]
    zs = []
    for shift in (0, -1, 1):
        at = (m + shift + count) % count
        zs += [h * count + at, (1 - h) * count + at]
    xs = [x for xp in range(2) for x in (2 * x_high + xp, 3 - 2 * x_high - xp)]
    return jnp.stack([x * SIZES["h"] * count + z for x in xs for z in zs]).astype(jnp.int32)


def product_kernel(here, place, *refs, pieces, outs):
    rows, hidden = refs[0].shape[1:]
    flat = jnp.concatenate([piece[0] for piece in refs[:pieces]])
    blocks = refs[pieces:-outs[0] * outs[1]]
    weights = jnp.concatenate([block[...].reshape(-1, hidden) for block in blocks])
    result = lax.dot_general(
        flat, weights, (((1,), (1,)), ((), ())), preferred_element_type=jnp.float32
    ).astype(jnp.bfloat16)
    rest = [result[k * rows:(k + 1) * rows] for k in range(pieces)]
    step = 1
    while step < pieces:
        flip = (place[0] // step) % 2 == 1
        rest = [jnp.where(flip, rest[k ^ step], rest[k]) for k in range(pieces)]
        step *= 2
    share = pieces if outs[0] > 1 else pieces // outs[1]
    for i, out in enumerate(refs[-outs[0] * outs[1]:]):
        part = i % outs[1]

        @pl.when(pl.program_id(0) == i // outs[1])
        def _():
            for k in range(share):
                out[k * rows:(k + 1) * rows, :] = rest[part * share + k]


def product(where, pieces, blocks, first, stride, count, parts=1):
    tensor_count, rows, hidden = pieces[0].shape
    rows_out = rows * len(pieces)
    outs = count * parts
    features = sum(block.shape[0] * block.shape[1] for block in blocks)
    flops = 2 * count * rows_out * hidden * features
    moved = 2 * (count * rows_out * (hidden + features) + features * hidden)

    def source(i, here, place):
        return ((here[0] + first + i * stride) % tensor_count, 0, 0)

    return pl.pallas_call(
        functools.partial(product_kernel, pieces=len(pieces), outs=(count, parts)),
        grid_spec=pltpu.PrefetchScalarGridSpec(
            num_scalar_prefetch=2,
            grid=(count,),
            in_specs=[pl.BlockSpec((1, rows, hidden), source)] * len(pieces)
            + [pl.BlockSpec(block.shape, lambda i, here, place: (0, 0, 0)) for block in blocks],
            out_specs=[pl.BlockSpec((rows_out // parts, features), lambda i, here, place: (0, 0))] * outs,
        ),
        out_shape=[jax.ShapeDtypeStruct((rows_out // parts, features), jnp.bfloat16)] * outs,
        cost_estimate=pl.CostEstimate(flops=flops, bytes_accessed=moved, transcendentals=0),
        compiler_params=pltpu.CompilerParams(vmem_limit_bytes=14 * 1024 * 1024),
    )(*where, *pieces, *blocks)


def add_kernel(*refs, at):
    *terms, out = refs
    base, came = terms[0], terms[1:]
    rows = came[0].shape[0]
    total = base[at:at + rows, :].astype(jnp.float32)
    for term in came:
        total += term[...].astype(jnp.float32)
    out[at:at + rows, :] = total.astype(out.dtype)
    for low, high in ((0, at), (at + rows, base.shape[0])):
        if low < high:
            out[low:high, :] = base[low:high, :]


def add(base, *came, at=0):
    vmem = pl.BlockSpec(memory_space=pltpu.VMEM)
    size = base.size
    return pl.pallas_call(
        functools.partial(add_kernel, at=at),
        out_shape=jax.ShapeDtypeStruct(base.shape, base.dtype),
        in_specs=[vmem] * (1 + len(came)),
        out_specs=vmem,
        cost_estimate=pl.CostEstimate(flops=size, bytes_accessed=6 * size, transcendentals=0),
        compiler_params=pltpu.CompilerParams(vmem_limit_bytes=8 * 1024 * 1024),
    )(base, *came)


def after(value, *others):
    anywhere = pl.BlockSpec(memory_space=pl.ANY)
    return pl.pallas_call(
        lambda *refs: None,
        out_shape=jax.ShapeDtypeStruct(value.shape, value.dtype),
        in_specs=[anywhere] * (1 + len(others)),
        out_specs=anywhere,
        input_output_aliases={0: 0},
        cost_estimate=pl.CostEstimate(flops=0, bytes_accessed=0, transcendentals=0),
        compiler_params=pltpu.CompilerParams(vmem_limit_bytes=1024 * 1024),
    )(value, *others)


def sum_by_arms(partial, n):
    mid = n // 2
    up = [(i, (i + 1) % n) for i in range(n)]
    down = [(i, (i - 1) % n) for i in range(n)]

    low, high = partial(mid, 1, 1, 2)
    first = lax.ppermute(low, "t", up)
    last = lax.ppermute(high, "t", down)
    above, below = partial(mid - 1, 2, 2, 1)
    going_up = add(above, first)
    going_down = add(below, last, at=low.shape[0])
    uppers, lowers = partial(mid - 2, -1, mid - 2, 1), partial(mid + 2, 1, mid - 1, 1)
    for step in range(1, mid):
        from_below = lax.ppermute(going_up, "t", up)
        from_above = lax.ppermute(going_down, "t", down)
        if step < mid - 1:
            going_up = add(uppers[step - 1], from_below)
            going_down = add(lowers[step - 1], from_above)
    return add(lowers[mid - 2], from_below, from_above)


def give_back(summed, owners, capacity):
    features = summed.shape[-1]
    got = lax.all_to_all(summed.reshape(-1, capacity, features), ("xp", "c", "e"), 0, 0)
    return got.reshape(-1, owners * capacity, features)


def place_kernel(places, onehot, piece, out, *, width):
    cores = SIZES["c"]
    count = piece.shape[2] // width
    for xp in range(SIZES["xp"]):
        for b in range(count):
            block = jnp.concatenate(
                [piece[xp * cores + c, :, b * width:(b + 1) * width] for c in range(cores)], axis=1
            )
            result = jnp.dot(onehot[...], block, preferred_element_type=jnp.float32)
            start = pl.multiple_of(places[xp * count + b] * (cores * width), cores * width)
            out[:, pl.ds(start, cores * width)] = result.astype(out.dtype)


def shards(routes, upgrad, weight):
    _, _, tensor_count, owners, capacity, hidden = upgrad.shape
    slab = weight[0]
    width = slab.shape[0]
    rows = owners * capacity

    own = upgrad.reshape(tensor_count, rows, hidden)
    x_rows = lax.ppermute(own, "xp", SWAP)
    c_rows = lax.ppermute(own, "c", SWAP)
    column, other = gather_columns(slab)
    x_rows = after(x_rows, *column, *other)
    pieces = (own, c_rows, x_rows, lax.ppermute(x_rows, "c", SWAP))

    places = [lax.axis_index("t"), lax.axis_index("xp") * SIZES["c"] + lax.axis_index("c")]
    where = [place.astype(jnp.int32).reshape(1) for place in places]
    blocks = (*column, *other)
    summed = sum_by_arms(
        lambda *at: product(where, pieces, blocks, *at), tensor_count
    )
    piece = give_back(summed, owners, capacity)

    owner_ids = lax.iota(jnp.int32, owners)
    is_routed = jnp.any(routes[:, :, None] == owner_ids[None, None, :], axis=1)
    slot_index = jnp.cumsum(is_routed.astype(jnp.int32), axis=0) - 1
    onehot = is_routed[:, :, None] & (slot_index[:, :, None] == lax.iota(jnp.int32, capacity)[None, None, :])
    onehot = onehot.reshape(routes.shape[0], rows).astype(jnp.bfloat16)

    def body(*refs):
        place_kernel(*refs, width=width)

    smem = pl.BlockSpec(memory_space=pltpu.SMEM)
    vmem = pl.BlockSpec(memory_space=pltpu.VMEM)
    total = piece.shape[0] * piece.shape[2]
    return pl.pallas_call(
        body,
        out_shape=jax.ShapeDtypeStruct((routes.shape[0], total), jnp.bfloat16),
        in_specs=[smem, vmem, vmem],
        out_specs=vmem,
        compiler_params=pltpu.CompilerParams(vmem_limit_bytes=8 * 1024 * 1024),
    )(block_places(), onehot, piece)


def solution(mesh):
    fine = Mesh(mesh.devices.reshape(tuple(SIZES.values())), tuple(SIZES))
    return jax.shard_map(
        shards,
        mesh=fine,
        in_specs=(
            P(DP + ("e", "t"), None),
            P(DP, "e", None, None, None, "t"),
            P("e", DP, "t"),
        ),
        out_specs=P(DP + ("e", "t"), None),
        check_vma=False,
    )
```

```python
import functools

import jax
import jax.numpy as jnp
from jax import lax
from jax.experimental import pallas as pl
from jax.experimental.pallas import tpu as pltpu
from jax.sharding import Mesh, PartitionSpec as P

SIZES = {"xh": 2, "xp": 2, "h": 2, "m": 3, "c": 2, "e": 2, "t": 8}
DP = ("xh", "xp", "h", "m", "c")
SWAP = [(0, 1), (1, 0)]
WEIGHT_SWAP = [(i, 3 - i) for i in range(4)]


def turn(shift):
    return [(i, (i + shift) % SIZES["m"]) for i in range(SIZES["m"])]


def gather_columns(slab):
    opposite = lambda value: lax.ppermute(value, ("xh", "xp"), WEIGHT_SWAP)
    pair = jnp.stack([slab, lax.ppermute(slab, "h", SWAP)])
    blocks = (pair, lax.ppermute(pair, "m", turn(1)), lax.ppermute(pair, "m", turn(-1)))
    return blocks, [opposite(block) for block in blocks]


def block_places():
    x_high, h, m = lax.axis_index("xh"), lax.axis_index("h"), lax.axis_index("m")
    count = SIZES["m"]
    zs = []
    for shift in (0, -1, 1):
        at = (m + shift + count) % count
        zs += [h * count + at, (1 - h) * count + at]
    xs = [x for xp in range(2) for x in (2 * x_high + xp, 3 - 2 * x_high - xp)]
    return jnp.stack([x * SIZES["h"] * count + z for x in xs for z in zs]).astype(jnp.int32)


def product_kernel(here, place, *refs, pieces, outs):
    rows, hidden = refs[0].shape[1:]
    flat = jnp.concatenate([piece[0] for piece in refs[:pieces]])
    blocks = refs[pieces:-outs[0] * outs[1]]
    weights = jnp.concatenate([block[...].reshape(-1, hidden) for block in blocks])
    result = lax.dot_general(
        flat, weights, (((1,), (1,)), ((), ())), preferred_element_type=jnp.float32
    ).astype(jnp.bfloat16)
    rest = [result[k * rows:(k + 1) * rows] for k in range(pieces)]
    step = 1
    while step < pieces:
        flip = (place[0] // step) % 2 == 1
        rest = [jnp.where(flip, rest[k ^ step], rest[k]) for k in range(pieces)]
        step *= 2
    share = pieces if outs[0] > 1 else pieces // outs[1]
    for i, out in enumerate(refs[-outs[0] * outs[1]:]):
        part = i % outs[1]

        @pl.when(pl.program_id(0) == i // outs[1])
        def _():
            for k in range(share):
                out[k * rows:(k + 1) * rows, :] = rest[part * share + k]


def product(where, pieces, blocks, first, stride, count, parts=1):
    tensor_count, rows, hidden = pieces[0].shape
    rows_out = rows * len(pieces)
    outs = count * parts
    features = sum(block.shape[0] * block.shape[1] for block in blocks)
    flops = 2 * count * rows_out * hidden * features
    moved = 2 * (count * rows_out * (hidden + features) + features * hidden)

    def source(i, here, place):
        return ((here[0] + first + i * stride) % tensor_count, 0, 0)

    return pl.pallas_call(
        functools.partial(product_kernel, pieces=len(pieces), outs=(count, parts)),
        grid_spec=pltpu.PrefetchScalarGridSpec(
            num_scalar_prefetch=2,
            grid=(count,),
            in_specs=[pl.BlockSpec((1, rows, hidden), source)] * len(pieces)
            + [pl.BlockSpec(block.shape, lambda i, here, place: (0, 0, 0)) for block in blocks],
            out_specs=[pl.BlockSpec((rows_out // parts, features), lambda i, here, place: (0, 0))] * outs,
        ),
        out_shape=[jax.ShapeDtypeStruct((rows_out // parts, features), jnp.bfloat16)] * outs,
        cost_estimate=pl.CostEstimate(flops=flops, bytes_accessed=moved, transcendentals=0),
        compiler_params=pltpu.CompilerParams(vmem_limit_bytes=14 * 1024 * 1024),
    )(*where, *pieces, *blocks)


def add_kernel(*refs, at):
    *terms, out = refs
    base, came = terms[0], terms[1:]
    rows = came[0].shape[0]
    total = base[at:at + rows, :].astype(jnp.float32)
    for term in came:
        total += term[...].astype(jnp.float32)
    out[at:at + rows, :] = total.astype(out.dtype)
    for low, high in ((0, at), (at + rows, base.shape[0])):
        if low < high:
            out[low:high, :] = base[low:high, :]


def add(base, *came, at=0):
    vmem = pl.BlockSpec(memory_space=pltpu.VMEM)
    size = base.size
    return pl.pallas_call(
        functools.partial(add_kernel, at=at),
        out_shape=jax.ShapeDtypeStruct(base.shape, base.dtype),
        in_specs=[vmem] * (1 + len(came)),
        out_specs=vmem,
        cost_estimate=pl.CostEstimate(flops=size, bytes_accessed=6 * size, transcendentals=0),
        compiler_params=pltpu.CompilerParams(vmem_limit_bytes=8 * 1024 * 1024),
    )(base, *came)


def after(value, *others):
    anywhere = pl.BlockSpec(memory_space=pl.ANY)
    return pl.pallas_call(
        lambda *refs: None,
        out_shape=jax.ShapeDtypeStruct(value.shape, value.dtype),
        in_specs=[anywhere] * (1 + len(others)),
        out_specs=anywhere,
        input_output_aliases={0: 0},
        cost_estimate=pl.CostEstimate(flops=0, bytes_accessed=0, transcendentals=0),
        compiler_params=pltpu.CompilerParams(vmem_limit_bytes=1024 * 1024),
    )(value, *others)


def sum_by_arms(partial, n):
    mid = n // 2
    up = [(i, (i + 1) % n) for i in range(n)]
    down = [(i, (i - 1) % n) for i in range(n)]

    low, high = partial(mid, 1, 1, 2)
    first = lax.ppermute(low, "t", up)
    last = lax.ppermute(high, "t", down)
    above, below = partial(mid - 1, 2, 2, 1)
    going_up = add(above, first)
    going_down = add(below, last, at=low.shape[0])
    uppers, lowers = partial(mid - 2, -1, mid - 2, 1), partial(mid + 2, 1, mid - 1, 1)
    for step in range(1, mid):
        from_below = lax.ppermute(going_up, "t", up)
        from_above = lax.ppermute(going_down, "t", down)
        if step < mid - 1:
            going_up = add(uppers[step - 1], from_below)
            going_down = add(lowers[step - 1], from_above)
    return add(lowers[mid - 2], from_below, from_above)


def give_back(summed, owners, capacity):
    features = summed.shape[-1]
    got = lax.all_to_all(summed.reshape(-1, capacity, features), ("xp", "c", "e"), 0, 0)
    return got.reshape(-1, owners * capacity, features)


def place_kernel(places, onehot, piece, out, *, width):
    cores = SIZES["c"]
    count = piece.shape[2] // width
    for xp in range(SIZES["xp"]):
        for b in range(count):
            block = jnp.concatenate(
                [piece[xp * cores + c, :, b * width:(b + 1) * width] for c in range(cores)], axis=1
            )
            result = jnp.dot(onehot[...], block, preferred_element_type=jnp.float32)
            start = pl.multiple_of(places[xp * count + b] * (cores * width), cores * width)
            out[:, pl.ds(start, cores * width)] = result.astype(out.dtype)


def shards(routes, upgrad, weight):
    _, _, tensor_count, owners, capacity, hidden = upgrad.shape
    slab = weight[0]
    width = slab.shape[0]
    rows = owners * capacity

    own = upgrad.reshape(tensor_count, rows, hidden)
    x_rows = lax.ppermute(own, "xp", SWAP)
    c_rows = lax.ppermute(own, "c", SWAP)
    column, other = gather_columns(slab)
    x_rows = after(x_rows, *column, *other)
    pieces = (after(own, column[0]), c_rows, x_rows, lax.ppermute(x_rows, "c", SWAP))

    places = [lax.axis_index("t"), lax.axis_index("xp") * SIZES["c"] + lax.axis_index("c")]
    where = [place.astype(jnp.int32).reshape(1) for place in places]
    blocks = (*column, *other)
    summed = sum_by_arms(
        lambda *at: product(where, pieces, blocks, *at), tensor_count
    )
    piece = give_back(summed, owners, capacity)

    owner_ids = lax.iota(jnp.int32, owners)
    is_routed = jnp.any(routes[:, :, None] == owner_ids[None, None, :], axis=1)
    slot_index = jnp.cumsum(is_routed.astype(jnp.int32), axis=0) - 1
    onehot = is_routed[:, :, None] & (slot_index[:, :, None] == lax.iota(jnp.int32, capacity)[None, None, :])
    onehot = onehot.reshape(routes.shape[0], rows).astype(jnp.bfloat16)

    def body(*refs):
        place_kernel(*refs, width=width)

    smem = pl.BlockSpec(memory_space=pltpu.SMEM)
    vmem = pl.BlockSpec(memory_space=pltpu.VMEM)
    total = piece.shape[0] * piece.shape[2]
    return pl.pallas_call(
        body,
        out_shape=jax.ShapeDtypeStruct((routes.shape[0], total), jnp.bfloat16),
        in_specs=[smem, vmem, vmem],
        out_specs=vmem,
        compiler_params=pltpu.CompilerParams(vmem_limit_bytes=8 * 1024 * 1024),
    )(block_places(), onehot, piece)


def solution(mesh):
    fine = Mesh(mesh.devices.reshape(tuple(SIZES.values())), tuple(SIZES))
    return jax.shard_map(
        shards,
        mesh=fine,
        in_specs=(
            P(DP + ("e", "t"), None),
            P(DP, "e", None, None, None, "t"),
            P("e", DP, "t"),
        ),
        out_specs=P(DP + ("e", "t"), None),
        check_vma=False,
    )
```
